256 devices in a mesh: blk: 64 (over x, z, core), pair: 4 (over y).
Axes of the slice: x: 4, y: 4, z: 8, core: 2. Of those that a mesh axis runs over, the one named last changes fastest.
Arguments:
- records: bfloat16 [64, 8192, 2048], P('blk', 'pair'), may hold values from -100 to 100
- offsets: int32 [2], replicated, may hold values from 1 to 15, as said below
- source_side: int32 [64, 2], P('blk'), may hold values from 0 to 1
Outputs:
- first_side: bfloat16 [64, 2, 32, 128, 128], P('blk', None, 'pair')
- second_side: bfloat16 [64, 2, 32, 128, 128], P('blk', None, 'pair')
The draws below stay inside these ranges and needn't reach their ends.
Inputs may be any that keep to these rules, and one draw needn't show every extreme that they name: `offsets`: distinct and increasing; the last one is 15.
All inputs are finite; a program needn't handle non-finite values.
Results may differ from the reference program's by a relative error of at most 0.012.
Values may be sent and summed in bfloat16 or wider, within the bound.
A program may use at most 128 MiB of HBM per device.

```python
import math
import jax
import jax.numpy as jnp
from jax import lax

BLOCK_CH = 128
BINS = 128
SAMPLES = 2048
FIRST_BIN = 4
LAGS = 32
OFFSET_COUNT = 2
WINDOW = 16
SEGMENTS = 64
BLOCKS = 64
CHANNELS = 8192


def draw_records(key, part):
    base_key = jax.random.fold_in(key, 101)
    noise_key, channel_key, segment_key = jax.random.split(base_key, 3)
    channel_scale = jnp.exp(jax.random.uniform(channel_key, (1, CHANNELS, 1), jnp.float32, 0.0, math.log(10.0)))
    segment_scale = jnp.exp(jax.random.uniform(segment_key, (SEGMENTS, 1, 1), jnp.float32, 0.0, math.log(4.0)))
    noise = jax.random.normal(noise_key, (SEGMENTS, CHANNELS, SAMPLES), jnp.float32)
    values = noise * channel_scale * segment_scale
    return jnp.clip(values, -100.0, 100.0).astype(jnp.bfloat16)


def draw_offsets(key, part):
    order_key = jax.random.fold_in(key, 202)
    shuffled = jax.random.permutation(order_key, WINDOW - 2).astype(jnp.int32) + 1
    chosen = jnp.sort(shuffled[:OFFSET_COUNT - 1])
    last_one = jnp.full((1,), WINDOW - 1, jnp.int32)
    return jnp.concatenate([chosen, last_one]).astype(jnp.int32)


def plant(array, stream_key, smallest, top_value):
    longest = array.shape.index(max(array.shape))
    spots = []
    for shift in (0, 1):
        where = [jax.random.randint(jax.random.fold_in(stream_key, axis), (), 0, length) for axis, length in enumerate(array.shape)]
        where[longest] = (where[longest] + shift) % array.shape[longest]
        spots.append(tuple(where))
    return array.at[spots[0]].set(smallest).at[spots[1]].set(top_value)


def setup_inputs(seed: int = 0) -> dict:
    key_of = jax.random.split(jax.random.key(seed), 4)
    return {
        "records": draw_records(jax.random.fold_in(key_of[3], 71), 0),
        "offsets": draw_offsets(jax.random.fold_in(key_of[3], 71), 0),
        "source_side": plant(jax.random.randint(key_of[2], (BLOCKS, OFFSET_COUNT), 0, 2), jax.random.fold_in(key_of[2], 1), 0, 1).astype(jnp.int32),
    }


def whiten_segment(segment):
    sample_index = jnp.arange(SAMPLES, dtype=jnp.float32)
    hann_taper = 0.5 - 0.5 * jnp.cos(2.0 * math.pi / SAMPLES * sample_index)
    tapered = segment.astype(jnp.float32) * hann_taper
    spectrum = jnp.fft.rfft(tapered, axis=-1)[:, FIRST_BIN:FIRST_BIN + BINS]
    real_part = jnp.real(spectrum).reshape(BLOCKS, BLOCK_CH, BINS)
    imag_part = jnp.imag(spectrum).reshape(BLOCKS, BLOCK_CH, BINS)
    band_level = lax.optimization_barrier(jnp.mean(real_part * real_part + imag_part * imag_part, axis=1, keepdims=True))
    whiten_scale = 1.0 / jnp.sqrt(band_level + 1e-05)
    return jnp.stack((real_part * whiten_scale, imag_part * whiten_scale)).astype(jnp.bfloat16)

def reference(records, offsets, source_side):
    whitened = lax.map(whiten_segment, records)
    lag_index = jnp.arange(LAGS, dtype=jnp.int32) - LAGS // 2
    bin_index = FIRST_BIN + jnp.arange(BINS, dtype=jnp.int32)
    phase_index = lag_index[:, None] * bin_index[None, :] % SAMPLES
    angles = 2.0 * math.pi / SAMPLES * phase_index.astype(jnp.float32)
    normalizer = 1.0 / jnp.sqrt(jnp.float32(SEGMENTS * BINS))
    cos_table = jnp.cos(angles) * normalizer
    sin_table = jnp.sin(angles) * normalizer
    highest = lax.Precision.HIGHEST

    def pair_block(block_index):
        own_block = lax.dynamic_index_in_dim(whitened, block_index, axis=2, keepdims=False)
        results = []
        for offset_slot in range(OFFSET_COUNT):
            partner = block_index + offsets[offset_slot]
            in_range = partner < BLOCKS
            partner_block = lax.dynamic_index_in_dim(whitened, jnp.minimum(partner, BLOCKS - 1).astype(jnp.int32), axis=2, keepdims=False)
            reverse_side = source_side[block_index, offset_slot] == 1
            source = jnp.where(reverse_side, partner_block, own_block).astype(jnp.float32)
            receiver = jnp.where(reverse_side, own_block, partner_block).astype(jnp.float32)
            cross_real = jnp.einsum('scf,sdf->fcd', source[:, 0], receiver[:, 0], precision=highest) + jnp.einsum('scf,sdf->fcd', source[:, 1], receiver[:, 1], precision=highest)
            cross_imag = jnp.einsum('scf,sdf->fcd', source[:, 0], receiver[:, 1], precision=highest) - jnp.einsum('scf,sdf->fcd', source[:, 1], receiver[:, 0], precision=highest)
            lagged = jnp.einsum('lf,fcd->lcd', cos_table, cross_real, precision=highest) - jnp.einsum('lf,fcd->lcd', sin_table, cross_imag, precision=highest)
            results.append(jnp.where(in_range, lagged, jnp.zeros_like(lagged)).astype(jnp.bfloat16))
        return jnp.stack(results)
    first_side = lax.map(pair_block, jnp.arange(BLOCKS, dtype=jnp.int32))
    seconds = []
    for offset_slot in range(OFFSET_COUNT):
        anchor = jnp.arange(BLOCKS, dtype=jnp.int32) - offsets[offset_slot]
        picked = jnp.take(first_side[:, offset_slot], jnp.maximum(anchor, 0).astype(jnp.int32), axis=0)
        seconds.append(jnp.where((anchor >= 0)[:, None, None, None], picked, jnp.zeros_like(picked)))
    second_side = jnp.stack(seconds, axis=1)
    return (first_side, second_side)
```

```python
import functools
import math

import jax
import jax.numpy as jnp
import numpy as np
from jax import lax
from jax.experimental import pallas as pl
from jax.experimental.pallas import tpu as pltpu
from jax.sharding import PartitionSpec as P

BLOCK_CH = 128
BINS = 128
SAMPLES = 2048
FIRST_BIN = 4
LAGS = 32
SEGMENTS = 64
BLOCKS = 64
LAST_OFFSET = 15
PAIRS = 4
BIN_LOCAL = BINS // PAIRS
ROWS = 2 * BIN_LOCAL
LAG_LOCAL = LAGS // PAIRS
LOCAL_BLOCKS = BLOCKS // PAIRS
GROUP = 2
GROUPS = LOCAL_BLOCKS // GROUP
TILE = 16
BF16 = jnp.bfloat16
F32 = jnp.float32
MESH = pl.DeviceIdType.MESH


def fourier_rows():
    n = np.arange(SAMPLES, dtype=np.int64)
    k = FIRST_BIN + np.arange(BINS, dtype=np.int64)
    angles = 2.0 * math.pi / SAMPLES * (k[:, None] * n[None, :] % SAMPLES).astype(np.float64)
    taper = 0.5 - 0.5 * np.cos(2.0 * math.pi / SAMPLES * n.astype(np.float64))
    table = np.stack((taper * np.cos(angles), -taper * np.sin(angles)))
    table = table.reshape(2, PAIRS, BIN_LOCAL, SAMPLES).transpose(1, 0, 2, 3).reshape(2 * BINS, SAMPLES)
    high = table.astype(BF16)
    low = (table - high.astype(np.float64)).astype(BF16)
    return np.concatenate((high, low), axis=0)


def lag_rows():
    lag = np.arange(LAGS, dtype=np.int64) - LAGS // 2
    k = FIRST_BIN + np.arange(BINS, dtype=np.int64)
    angles = 2.0 * math.pi / SAMPLES * (lag[:, None] * k[None, :] % SAMPLES).astype(np.float64)
    table = np.stack((np.cos(angles), -np.sin(angles))) / math.sqrt(SEGMENTS * BINS)
    table = table.reshape(2, LAGS, PAIRS, BIN_LOCAL).transpose(2, 1, 0, 3).reshape(PAIRS, LAGS, ROWS)
    same = np.eye(TILE)
    spread = table[:, :, None, :, None] * same[None, None, :, None, :]
    return spread.reshape(PAIRS, LAGS * TILE, ROWS * TILE).astype(BF16)


def swap_rows():
    index = np.arange(TILE * TILE)
    table = np.zeros((TILE * TILE, TILE * TILE))
    table[index, (index % TILE) * TILE + index // TILE] = 1.0
    return table.astype(BF16)


def kernel(
    records, fourier, lagtab, swap, offsets, sides,
    first, second,
    rec_v, fourier_v, lagtab_v, swap_v,
    shares, spectra, staged, own, far, near, own_t, far_t, cross, lagged, arrived,
    load_sem, table_sem, ys, yr, own_s, own_r, near_s, near_r, far_s, far_r, here_sem, lag_s, lag_r, sec_s, sec_r,
):
    me = lax.axis_index("blk")
    q = lax.axis_index("pair")
    barrier = pltpu.get_barrier_semaphore()

    loads = []
    table_loads = [
        pltpu.make_async_copy(fourier, fourier_v, table_sem.at[0]),
        pltpu.make_async_copy(swap, swap_v, table_sem.at[1]),
        pltpu.make_async_copy(lagtab.at[q], lagtab_v, table_sem.at[2]),
    ]
    table_loads[0].start()
    width = GROUP * BLOCK_CH
    for g in range(GROUPS):
        copy = pltpu.make_async_copy(records.at[0, pl.ds(g * width, width)], rec_v.at[g], load_sem.at[g])
        copy.start()
        loads.append(copy)
    table_loads[1].start()
    table_loads[2].start()

    def greet(t, carry):
        pl.semaphore_signal(barrier, inc=1, device_id=(lax.rem(me + t, BLOCKS), q), device_id_type=MESH)
        return carry

    lax.fori_loop(1, BLOCKS, greet, 0)
    for t in range(1, PAIRS):
        pl.semaphore_signal(barrier, inc=1, device_id=(me, lax.rem(q + t, PAIRS)), device_id_type=MESH)

    def whiten(g):
        out = lax.dot_general(
            fourier_v[...], rec_v[g], (((1,), (1,)), ((), ())), preferred_element_type=F32
        )
        spectrum = (out[: 2 * BINS] + out[2 * BINS :]).reshape(PAIRS, 2, BIN_LOCAL, width)
        power = spectrum[:, 0] * spectrum[:, 0] + spectrum[:, 1] * spectrum[:, 1]
        for i in range(GROUP):
            lanes = slice(i * BLOCK_CH, (i + 1) * BLOCK_CH)
            level = jnp.sum(power[:, :, lanes], axis=-1, keepdims=True) * (1.0 / BLOCK_CH)
            scale = 1.0 / jnp.sqrt(level + 1e-05)
            white = (spectrum[:, :, :, lanes] * scale[:, None]).astype(BF16)
            shares[:, g * GROUP + i] = white.reshape(PAIRS, ROWS, BLOCK_CH)
            spectra[q * LOCAL_BLOCKS + g * GROUP + i] = shares[q, g * GROUP + i]

    def send_block(source, target, b, send_sem, recv_sem):
        @pl.when(b != me)
        def _():
            pltpu.make_async_remote_copy(
                src_ref=source.at[b], dst_ref=target.at[me], send_sem=send_sem, recv_sem=recv_sem,
                device_id=(b, q), device_id_type=MESH,
            ).start()

    def send_group(g):
        for t in range(1, PAIRS):
            peer = lax.rem(q + t, PAIRS)
            pltpu.make_async_remote_copy(
                src_ref=shares.at[peer, pl.ds(g * GROUP, GROUP)],
                dst_ref=spectra.at[pl.ds(q * LOCAL_BLOCKS + g * GROUP, GROUP)],
                send_sem=ys.at[t], recv_sem=yr.at[t],
                device_id=(me, peer), device_id_type=MESH,
            ).start()
        for i in range(GROUP):
            send_block(spectra, own, q * LOCAL_BLOCKS + g * GROUP + i, own_s, own_r)

    table_loads[0].wait()
    loads[0].wait()
    whiten(0)
    pl.semaphore_wait(barrier, BLOCKS - 1 + PAIRS - 1)
    send_group(0)
    for g in range(1, GROUPS):
        loads[g].wait()

    def group_step(g, carry):
        whiten(g)
        send_group(g)
        return carry

    lax.fori_loop(1, GROUPS, group_step, 0)

    sixteen = spectra.at[pl.ds(0, LOCAL_BLOCKS)]
    for t in (1, 3, 2):
        pltpu.make_async_copy(sixteen, sixteen, yr.at[t]).wait()
        base = lax.rem(q + PAIRS - t, PAIRS) * LOCAL_BLOCKS

        def send_quarter(m, carry):
            send_block(spectra, own, base + lax.rem(m + me, LOCAL_BLOCKS), own_s, own_r)
            return carry

        lax.fori_loop(0, LOCAL_BLOCKS, send_quarter, 0)
    own_here = pltpu.make_async_copy(spectra.at[me], own.at[me], here_sem.at[0])
    own_here.start()

    offset = offsets[0]

    def stage(b, carry):
        staged[b] = spectra[jnp.minimum(b + offset, BLOCKS - 1)]
        return carry

    lax.fori_loop(0, BLOCKS, stage, 0)
    near_here = pltpu.make_async_copy(staged.at[me], near.at[me], here_sem.at[1])
    near_here.start()

    def send_staged(t, carry):
        b = lax.rem(me + t, BLOCKS)
        pltpu.make_async_remote_copy(
            src_ref=staged.at[b], dst_ref=near.at[me], send_sem=near_s, recv_sem=near_r,
            device_id=(b, q), device_id_type=MESH,
        ).start()
        return carry

    lax.fori_loop(1, BLOCKS, send_staged, 0)

    others = own.at[pl.ds(0, BLOCKS - 1)]
    table_loads[1].wait()
    table_loads[2].wait()
    own_here.wait()
    pltpu.make_async_copy(others, others, own_r).wait()
    forward = pltpu.make_async_remote_copy(
        src_ref=own, dst_ref=far, send_sem=far_s, recv_sem=far_r,
        device_id=(lax.rem(me + BLOCKS - LAST_OFFSET, BLOCKS), q), device_id_type=MESH,
    )
    forward.start()

    def turn(source, target):
        def step(i, carry):
            s0 = pl.multiple_of(i // 4 * TILE, TILE)
            f0 = pl.multiple_of(i % 4 * TILE, TILE)
            tile = source[pl.ds(s0, TILE), pl.ds(f0, TILE), :].reshape(TILE * TILE, BLOCK_CH)
            turned = jnp.dot(swap_v[...], tile, preferred_element_type=F32).astype(BF16)
            target[pl.ds(f0, TILE), pl.ds(s0, TILE), :] = turned.reshape(TILE, TILE, BLOCK_CH)
            return carry

        lax.fori_loop(0, (SEGMENTS // TILE) * (ROWS // TILE), step, 0)

    turn(own, own_t)

    def correlate(k):
        side = sides[0, k].astype(F32)
        swapped = jnp.full((SEGMENTS, BLOCK_CH), side, F32).astype(BF16)
        straight = jnp.full((SEGMENTS, BLOCK_CH), 1.0 - side, F32).astype(BF16)

        def bin_step(f, carry):
            own_re, own_im = own_t[f], own_t[BIN_LOCAL + f]
            far_re, far_im = far_t[f], far_t[BIN_LOCAL + f]
            src_re = own_re * straight + far_re * swapped
            src_im = own_im * straight + far_im * swapped
            rec_re = far_re * straight + own_re * swapped
            rec_im = far_im * straight + own_im * swapped
            left = jnp.concatenate((src_re, src_im), axis=0)
            right = jnp.concatenate(
                (jnp.concatenate((rec_re, rec_im), axis=0), jnp.concatenate((rec_im, -rec_re), axis=0)), axis=1
            )
            out = lax.dot_general(left, right, (((0,), (0,)), ((), ())), preferred_element_type=F32)
            cross[f] = out[:, :BLOCK_CH].astype(BF16)
            cross[BIN_LOCAL + f] = out[:, BLOCK_CH:].astype(BF16)
            return carry

        lax.fori_loop(0, BIN_LOCAL, bin_step, 0)

        def lag_step(i, carry):
            c0 = pl.multiple_of(i * 2 * TILE, 2 * TILE)
            c1 = pl.multiple_of(i * 2 * TILE + TILE, TILE)
            cols = jnp.concatenate(
                (
                    cross[:, pl.ds(c0, TILE), :].reshape(ROWS * TILE, BLOCK_CH),
                    cross[:, pl.ds(c1, TILE), :].reshape(ROWS * TILE, BLOCK_CH),
                ),
                axis=1,
            )
            out = jnp.dot(lagtab_v[...], cols, preferred_element_type=F32).astype(BF16)
            lagged[k, :, pl.ds(c0, TILE), :] = out[:, :BLOCK_CH].reshape(LAGS, TILE, BLOCK_CH)
            lagged[k, :, pl.ds(c1, TILE), :] = out[:, BLOCK_CH:].reshape(LAGS, TILE, BLOCK_CH)
            return carry

        lax.fori_loop(0, BLOCK_CH // (2 * TILE), lag_step, 0)
        copies = []
        for t in (2, 1, 3):
            peer = lax.rem(q + t, PAIRS)
            copy = pltpu.make_async_remote_copy(
                src_ref=lagged.at[k, pl.ds(peer * LAG_LOCAL, LAG_LOCAL)], dst_ref=arrived.at[k, t],
                send_sem=lag_s.at[k, t], recv_sem=lag_r.at[k, t],
                device_id=(me, peer), device_id_type=MESH,
            )
            copy.start()
            copies.append(copy)
        return copies

    def finish(k, copies, keep):
        for copy in copies:
            copy.wait_recv()
        factor = keep.astype(F32)

        def lag_sum(l, carry):
            total = lagged[k, q * LAG_LOCAL + l].astype(F32)
            for t in range(1, PAIRS):
                total = total + arrived[k, t, l].astype(F32)
            first[k, l] = (total * factor).astype(BF16)
            return carry

        lax.fori_loop(0, LAG_LOCAL, lag_sum, 0)

    forward.wait_recv()
    turn(far, far_t)
    last_copies = correlate(1)

    near_here.wait()
    pltpu.make_async_copy(others, others, near_r).wait()
    turn(near, far_t)
    near_copies = correlate(0)

    finish(1, last_copies, jnp.where(me + LAST_OFFSET < BLOCKS, 1, 0))
    back = pltpu.make_async_remote_copy(
        src_ref=first.at[1], dst_ref=second, send_sem=sec_s, recv_sem=sec_r,
        device_id=(lax.rem(me + LAST_OFFSET, BLOCKS), q), device_id_type=MESH,
    )
    back.start()
    finish(0, near_copies, jnp.where(me + offset < BLOCKS, 1, 0))
    back.wait_recv()

    for t in range(1, PAIRS):
        pltpu.make_async_copy(sixteen, sixteen, ys.at[t]).wait()
    pltpu.make_async_copy(others, others, own_s).wait()
    pltpu.make_async_copy(others, others, near_s).wait()
    forward.wait_send()
    for copy in last_copies + near_copies:
        copy.wait_send()
    back.wait_send()


def correlations(records, offsets, sides):
    any_space = pl.BlockSpec(memory_space=pl.ANY)
    scalars = pl.BlockSpec(memory_space=pltpu.SMEM)
    vmem = pl.BlockSpec(memory_space=pltpu.VMEM)
    whole = (BLOCKS, ROWS, BLOCK_CH)
    dma = pltpu.SemaphoreType.DMA
    return pl.pallas_call(
        kernel,
        name="correlations",
        out_shape=(
            jax.ShapeDtypeStruct((2, LAG_LOCAL, BLOCK_CH, BLOCK_CH), BF16),
            jax.ShapeDtypeStruct((LAG_LOCAL, BLOCK_CH, BLOCK_CH), BF16),
        ),
        in_specs=[any_space] * 4 + [scalars] * 2,
        out_specs=(vmem, vmem),
        scratch_shapes=[
            pltpu.VMEM((GROUPS, GROUP * BLOCK_CH, SAMPLES), BF16),
            pltpu.VMEM((4 * BINS, SAMPLES), BF16),
            pltpu.VMEM((LAGS * TILE, ROWS * TILE), BF16),
            pltpu.VMEM((TILE * TILE, TILE * TILE), BF16),
            pltpu.VMEM((PAIRS, LOCAL_BLOCKS, ROWS, BLOCK_CH), BF16),
            pltpu.VMEM(whole, BF16),
            pltpu.VMEM(whole, BF16),
            pltpu.VMEM(whole, BF16),
            pltpu.VMEM(whole, BF16),
            pltpu.VMEM(whole, BF16),
            pltpu.VMEM((ROWS, SEGMENTS, BLOCK_CH), BF16),
            pltpu.VMEM((ROWS, SEGMENTS, BLOCK_CH), BF16),
            pltpu.VMEM((ROWS, BLOCK_CH, BLOCK_CH), BF16),
            pltpu.VMEM((2, LAGS, BLOCK_CH, BLOCK_CH), BF16),
            pltpu.VMEM((2, PAIRS, LAG_LOCAL, BLOCK_CH, BLOCK_CH), BF16),
            dma((GROUPS,)), dma((3,)), dma((PAIRS,)), dma((PAIRS,)),
            dma, dma, dma, dma, dma, dma, dma((2,)), dma((2, PAIRS)), dma((2, PAIRS)), dma, dma,
        ],
        compiler_params=pltpu.CompilerParams(
            collective_id=0, has_side_effects=True, vmem_limit_bytes=48 * 1024 * 1024
        ),
    )(records, jnp.asarray(fourier_rows()), jnp.asarray(lag_rows()), jnp.asarray(swap_rows()), offsets, sides)


def moved_ahead(steps):
    return lambda value: lax.ppermute(value, "blk", [(b, b + steps) for b in range(BLOCKS - steps)])


def local(records, offsets, sides):
    first, second_last = correlations(records, offsets, sides)
    second_near = lax.switch(offsets[0] - 1, [moved_ahead(steps) for steps in range(1, LAST_OFFSET)], first[0])
    return first[None], jnp.stack((second_near, second_last))[None]


def solution(mesh):
    return jax.shard_map(
        local,
        mesh=mesh,
        in_specs=(P("blk", "pair", None), P(), P("blk", None)),
        out_specs=(P("blk", None, "pair", None, None), P("blk", None, "pair", None, None)),
        check_vma=False,
    )
```

```python
import functools
import math

import jax
import jax.numpy as jnp
import numpy as np
from jax import lax
from jax.experimental import pallas as pl
from jax.experimental.pallas import tpu as pltpu
from jax.sharding import PartitionSpec as P

BLOCK_CH = 128
BINS = 128
SAMPLES = 2048
FIRST_BIN = 4
LAGS = 32
SEGMENTS = 64
BLOCKS = 64
LAST_OFFSET = 15
PAIRS = 4
BIN_LOCAL = BINS // PAIRS
ROWS = 2 * BIN_LOCAL
LAG_LOCAL = LAGS // PAIRS
LOCAL_BLOCKS = BLOCKS // PAIRS
GROUP = 2
GROUPS = LOCAL_BLOCKS // GROUP
BEHIND = 4
TILE = 16
BF16 = jnp.bfloat16
F32 = jnp.float32
MESH = pl.DeviceIdType.MESH


def fourier_rows():
    n = np.arange(SAMPLES, dtype=np.int64)
    k = FIRST_BIN + np.arange(BINS, dtype=np.int64)
    angles = 2.0 * math.pi / SAMPLES * (k[:, None] * n[None, :] % SAMPLES).astype(np.float64)
    taper = 0.5 - 0.5 * np.cos(2.0 * math.pi / SAMPLES * n.astype(np.float64))
    table = np.stack((taper * np.cos(angles), -taper * np.sin(angles)))
    table = table.reshape(2, PAIRS, BIN_LOCAL, SAMPLES).transpose(1, 0, 2, 3).reshape(2 * BINS, SAMPLES)
    high = table.astype(BF16)
    low = (table - high.astype(np.float64)).astype(BF16)
    return np.concatenate((high, low), axis=0)


def lag_rows():
    lag = np.arange(LAGS, dtype=np.int64) - LAGS // 2
    k = FIRST_BIN + np.arange(BINS, dtype=np.int64)
    angles = 2.0 * math.pi / SAMPLES * (lag[:, None] * k[None, :] % SAMPLES).astype(np.float64)
    table = np.stack((np.cos(angles), -np.sin(angles))) / math.sqrt(SEGMENTS * BINS)
    table = table.reshape(2, LAGS, PAIRS, BIN_LOCAL).transpose(2, 1, 0, 3).reshape(PAIRS, LAGS, ROWS)
    same = np.eye(TILE)
    spread = table[:, :, None, :, None] * same[None, None, :, None, :]
    return spread.reshape(PAIRS, LAGS * TILE, ROWS * TILE).astype(BF16)


def swap_rows():
    index = np.arange(TILE * TILE)
    table = np.zeros((TILE * TILE, TILE * TILE))
    table[index, (index % TILE) * TILE + index // TILE] = 1.0
    return table.astype(BF16)


def kernel(
    records, fourier, lagtab, swap, offsets_h, sides_h,
    first, second,
    rec_v, fourier_v, lagtab_v, swap_v, offsets, sides,
    shares, spectra, staged, own, far, near, own_t, far_t, cross, lagged, arrived, middle, onward,
    load_sem, table_sem, ys, yr, own_s, own_r, near_s, near_r, far_s, far_r, here_sem, lag_s, lag_r, sec_s, sec_r,
    mid_s, mid_r, out_s, out_r,
):
    me = lax.axis_index("blk")
    q = lax.axis_index("pair")
    barrier = pltpu.get_barrier_semaphore()

    loads = []
    table_loads = [
        pltpu.make_async_copy(fourier, fourier_v, table_sem.at[0]),
        pltpu.make_async_copy(swap, swap_v, table_sem.at[1]),
        pltpu.make_async_copy(lagtab.at[q], lagtab_v, table_sem.at[2]),
        pltpu.make_async_copy(offsets_h, offsets, table_sem.at[3]),
        pltpu.make_async_copy(sides_h, sides, table_sem.at[4]),
    ]
    table_loads[0].start()
    width = GROUP * BLOCK_CH
    place = lax.rem(me // 2, GROUPS)

    def turn_of(g):
        ahead = (g % 2) * ((g + 1) // 2) + (1 - g % 2) * (GROUPS - g // 2)
        return lax.rem(place + ahead, GROUPS)

    for g in range(GROUPS):
        row = pl.multiple_of(turn_of(g) * width, width)
        copy = pltpu.make_async_copy(records.at[0, pl.ds(row, width)], rec_v.at[g], load_sem.at[g])
        copy.start()
        loads.append(copy)
    for copy in table_loads[1:]:
        copy.start()

    def greet(t, carry):
        pl.semaphore_signal(barrier, inc=1, device_id=(lax.rem(me + t, BLOCKS), q), device_id_type=MESH)
        return carry

    lax.fori_loop(1, BLOCKS, greet, 0)
    for t in range(1, PAIRS):
        pl.semaphore_signal(barrier, inc=1, device_id=(me, lax.rem(q + t, PAIRS)), device_id_type=MESH)

    def whiten(g):
        out = lax.dot_general(
            fourier_v[...], rec_v[g], (((1,), (1,)), ((), ())), preferred_element_type=F32
        )
        spectrum = (out[: 2 * BINS] + out[2 * BINS :]).reshape(PAIRS, 2, BIN_LOCAL, width)
        at = turn_of(g) * GROUP
        power = spectrum[:, 0] * spectrum[:, 0] + spectrum[:, 1] * spectrum[:, 1]
        for i in range(GROUP):
            lanes = slice(i * BLOCK_CH, (i + 1) * BLOCK_CH)
            level = jnp.sum(power[:, :, lanes], axis=-1, keepdims=True) * (1.0 / BLOCK_CH)
            scale = 1.0 / jnp.sqrt(level + 1e-05)
            white = (spectrum[:, :, :, lanes] * scale[:, None]).astype(BF16)
            shares[:, at + i] = white.reshape(PAIRS, ROWS, BLOCK_CH)
            spectra[q * LOCAL_BLOCKS + at + i] = shares[q, at + i]

    def send_block(source, target, b, send_sem, recv_sem):
        @pl.when(b != me)
        def _():
            pltpu.make_async_remote_copy(
                src_ref=source.at[b], dst_ref=target.at[me], send_sem=send_sem, recv_sem=recv_sem,
                device_id=(b, q), device_id_type=MESH,
            ).start()

    def send_group(g):
        at = turn_of(g) * GROUP
        for t in (2, 1, 3):
            peer = lax.rem(q + t, PAIRS)
            pltpu.make_async_remote_copy(
                src_ref=shares.at[peer, pl.ds(at, GROUP)],
                dst_ref=spectra.at[pl.ds(q * LOCAL_BLOCKS + at, GROUP)],
                send_sem=ys.at[t], recv_sem=yr.at[t, g],
                device_id=(me, peer), device_id_type=MESH,
            ).start()
        for i in range(GROUP):
            send_block(spectra, own, q * LOCAL_BLOCKS + at + i, own_s, own_r)

    def pass_on(g):
        at = turn_of(g) * GROUP
        two = spectra.at[pl.ds(0, GROUP)]
        for t in (1, 3, 2):
            pltpu.make_async_copy(two, two, yr.at[t, g]).wait()
            base = lax.rem(q + PAIRS - t, PAIRS) * LOCAL_BLOCKS
            for i in range(GROUP):
                send_block(spectra, own, base + at + i, own_s, own_r)

    table_loads[0].wait()
    loads[0].wait()
    whiten(0)
    pl.semaphore_wait(barrier, BLOCKS - 1 + PAIRS - 1)
    send_group(0)
    for g in range(1, GROUPS):
        loads[g].wait()

    def group_step(g, carry):
        whiten(g)
        send_group(g)
        return carry

    def late_step(g, carry):
        whiten(g)
        send_group(g)
        pass_on(g - BEHIND)
        return carry

    def pass_step(g, carry):
        pass_on(g)
        return carry

    lax.fori_loop(1, BEHIND, group_step, 0)
    lax.fori_loop(BEHIND, GROUPS, late_step, 0)
    lax.fori_loop(GROUPS - BEHIND, GROUPS, pass_step, 0)
    sixteen = spectra.at[pl.ds(0, LOCAL_BLOCKS)]
    own_here = pltpu.make_async_copy(spectra.at[me], own.at[me], here_sem.at[0])
    own_here.start()

    for copy in table_loads[1:]:
        copy.wait()
    offset = offsets[0]

    def alternate(t):
        ahead = (t % 2) * ((t + 1) // 2) + (1 - t % 2) * (BLOCKS - t // 2)
        return lax.rem(me + ahead, BLOCKS)

    def stage(b, carry):
        staged[b] = spectra[jnp.minimum(b + offset, BLOCKS - 1)]
        return carry

    lax.fori_loop(0, BLOCKS, stage, 0)
    near_here = pltpu.make_async_copy(staged.at[me], near.at[me], here_sem.at[1])
    near_here.start()

    def send_staged(t, carry):
        b = alternate(t)
        pltpu.make_async_remote_copy(
            src_ref=staged.at[b], dst_ref=near.at[me], send_sem=near_s, recv_sem=near_r,
            device_id=(b, q), device_id_type=MESH,
        ).start()
        return carry

    lax.fori_loop(1, BLOCKS, send_staged, 0)

    others = own.at[pl.ds(0, BLOCKS - 1)]
    own_here.wait()
    pltpu.make_async_copy(others, others, own_r).wait()
    forward = pltpu.make_async_remote_copy(
        src_ref=own, dst_ref=far, send_sem=far_s, recv_sem=far_r,
        device_id=(lax.rem(me + BLOCKS - LAST_OFFSET, BLOCKS), q), device_id_type=MESH,
    )
    forward.start()

    def turn(source, target):
        def step(i, carry):
            s0 = pl.multiple_of(i // 4 * TILE, TILE)
            f0 = pl.multiple_of(i % 4 * TILE, TILE)
            tile = source[pl.ds(s0, TILE), pl.ds(f0, TILE), :].reshape(TILE * TILE, BLOCK_CH)
            turned = jnp.dot(swap_v[...], tile, preferred_element_type=F32).astype(BF16)
            target[pl.ds(f0, TILE), pl.ds(s0, TILE), :] = turned.reshape(TILE, TILE, BLOCK_CH)
            return carry

        lax.fori_loop(0, (SEGMENTS // TILE) * (ROWS // TILE), step, 0)

    turn(own, own_t)

    def correlate(k):
        side = sides[0, k].astype(F32)
        swapped = jnp.full((SEGMENTS, BLOCK_CH), side, F32).astype(BF16)
        straight = jnp.full((SEGMENTS, BLOCK_CH), 1.0 - side, F32).astype(BF16)

        def bin_step(f, carry):
            own_re, own_im = own_t[f], own_t[BIN_LOCAL + f]
            far_re, far_im = far_t[f], far_t[BIN_LOCAL + f]
            src_re = own_re * straight + far_re * swapped
            src_im = own_im * straight + far_im * swapped
            rec_re = far_re * straight + own_re * swapped
            rec_im = far_im * straight + own_im * swapped
            left = jnp.concatenate((src_re, src_im), axis=0)
            right = jnp.concatenate(
                (jnp.concatenate((rec_re, rec_im), axis=0), jnp.concatenate((rec_im, -rec_re), axis=0)), axis=1
            )
            out = lax.dot_general(left, right, (((0,), (0,)), ((), ())), preferred_element_type=F32)
            cross[f] = out[:, :BLOCK_CH].astype(BF16)
            cross[BIN_LOCAL + f] = out[:, BLOCK_CH:].astype(BF16)
            return carry

        lax.fori_loop(0, BIN_LOCAL, bin_step, 0)

        def lag_step(i, carry):
            c0 = pl.multiple_of(i * 2 * TILE, 2 * TILE)
            c1 = pl.multiple_of(i * 2 * TILE + TILE, TILE)
            cols = jnp.concatenate(
                (
                    cross[:, pl.ds(c0, TILE), :].reshape(ROWS * TILE, BLOCK_CH),
                    cross[:, pl.ds(c1, TILE), :].reshape(ROWS * TILE, BLOCK_CH),
                ),
                axis=1,
            )
            out = jnp.dot(lagtab_v[...], cols, preferred_element_type=F32).astype(BF16)
            lagged[k, :, pl.ds(c0, TILE), :] = out[:, :BLOCK_CH].reshape(LAGS, TILE, BLOCK_CH)
            lagged[k, :, pl.ds(c1, TILE), :] = out[:, BLOCK_CH:].reshape(LAGS, TILE, BLOCK_CH)
            return carry

        lax.fori_loop(0, BLOCK_CH // (2 * TILE), lag_step, 0)
        copies = []
        for t in (2, 1, 3):
            peer = lax.rem(q + t, PAIRS)
            copy = pltpu.make_async_remote_copy(
                src_ref=lagged.at[k, pl.ds(peer * LAG_LOCAL, LAG_LOCAL)], dst_ref=arrived.at[k, t],
                send_sem=lag_s.at[k, t], recv_sem=lag_r.at[k, t],
                device_id=(me, peer), device_id_type=MESH,
            )
            copy.start()
            copies.append(copy)
        return copies

    def finish(k, copies, keep):
        for copy in copies:
            copy.wait_recv()
        factor = keep.astype(F32)

        def lag_sum(l, carry):
            total = lagged[k, q * LAG_LOCAL + l].astype(F32)
            for t in range(1, PAIRS):
                total = total + arrived[k, t, l].astype(F32)
            first[k, l] = (total * factor).astype(BF16)
            return carry

        lax.fori_loop(0, LAG_LOCAL, lag_sum, 0)

    near_here.wait()
    pltpu.make_async_copy(others, others, near_r).wait()
    turn(near, far_t)
    near_copies = correlate(0)

    forward.wait_recv()
    turn(far, far_t)
    last_copies = correlate(1)

    def part(ref, m):
        return ref.at[0, m // 8, pl.ds(pl.multiple_of(m % 8 * TILE, TILE), TILE)]

    finish(0, near_copies, jnp.where(me + offset < BLOCKS, 1, 0))
    mid_here = pltpu.make_async_copy(part(first, me), middle.at[me], here_sem.at[2])
    mid_here.start()

    def send_part(t, carry):
        m = alternate(t)
        pltpu.make_async_remote_copy(
            src_ref=part(first, m), dst_ref=middle.at[me], send_sem=mid_s, recv_sem=mid_r,
            device_id=(m, q), device_id_type=MESH,
        ).start()
        return carry

    lax.fori_loop(1, BLOCKS, send_part, 0)

    finish(1, last_copies, jnp.where(me + LAST_OFFSET < BLOCKS, 1, 0))
    back = pltpu.make_async_remote_copy(
        src_ref=first.at[1], dst_ref=second.at[1], send_sem=sec_s, recv_sem=sec_r,
        device_id=(lax.rem(me + LAST_OFFSET, BLOCKS), q), device_id_type=MESH,
    )
    back.start()

    parts = middle.at[pl.ds(0, BLOCKS - 1)]
    mid_here.wait()
    pltpu.make_async_copy(parts, parts, mid_r).wait()

    def stage_part(j, carry):
        onward[j] = middle[lax.rem(j + BLOCKS - offset, BLOCKS)]
        return carry

    lax.fori_loop(0, BLOCKS, stage_part, 0)
    out_here = pltpu.make_async_copy(onward.at[me], part(second, me), here_sem.at[3])
    out_here.start()

    def send_onward(t, carry):
        j = alternate(t)
        pltpu.make_async_remote_copy(
            src_ref=onward.at[j], dst_ref=part(second, me), send_sem=out_s, recv_sem=out_r,
            device_id=(j, q), device_id_type=MESH,
        ).start()
        return carry

    lax.fori_loop(1, BLOCKS, send_onward, 0)
    out_here.wait()
    pltpu.make_async_copy(parts, parts, out_r).wait()
    back.wait_recv()

    for t in range(1, PAIRS):
        pltpu.make_async_copy(sixteen, sixteen, ys.at[t]).wait()
    pltpu.make_async_copy(others, others, own_s).wait()
    pltpu.make_async_copy(others, others, near_s).wait()
    forward.wait_send()
    for copy in last_copies + near_copies:
        copy.wait_send()
    back.wait_send()
    pltpu.make_async_copy(parts, parts, mid_s).wait()
    pltpu.make_async_copy(parts, parts, out_s).wait()


def correlations(records, offsets, sides):
    hbm = pl.BlockSpec(memory_space=pltpu.HBM)
    vmem = pl.BlockSpec(memory_space=pltpu.VMEM)
    whole = (BLOCKS, ROWS, BLOCK_CH)
    dma = pltpu.SemaphoreType.DMA
    return pl.pallas_call(
        kernel,
        name="correlations",
        out_shape=(
            jax.ShapeDtypeStruct((2, LAG_LOCAL, BLOCK_CH, BLOCK_CH), BF16),
            jax.ShapeDtypeStruct((2, LAG_LOCAL, BLOCK_CH, BLOCK_CH), BF16),
        ),
        in_specs=[hbm] * 6,
        out_specs=(vmem, vmem),
        scratch_shapes=[
            pltpu.VMEM((GROUPS, GROUP * BLOCK_CH, SAMPLES), BF16),
            pltpu.VMEM((4 * BINS, SAMPLES), BF16),
            pltpu.VMEM((LAGS * TILE, ROWS * TILE), BF16),
            pltpu.VMEM((TILE * TILE, TILE * TILE), BF16),
            pltpu.SMEM((2,), jnp.int32),
            pltpu.SMEM((1, 2), jnp.int32),
            pltpu.VMEM((PAIRS, LOCAL_BLOCKS, ROWS, BLOCK_CH), BF16),
            pltpu.VMEM(whole, BF16),
            pltpu.VMEM(whole, BF16),
            pltpu.VMEM(whole, BF16),
            pltpu.VMEM(whole, BF16),
            pltpu.VMEM(whole, BF16),
            pltpu.VMEM((ROWS, SEGMENTS, BLOCK_CH), BF16),
            pltpu.VMEM((ROWS, SEGMENTS, BLOCK_CH), BF16),
            pltpu.VMEM((ROWS, BLOCK_CH, BLOCK_CH), BF16),
            pltpu.VMEM((2, LAGS, BLOCK_CH, BLOCK_CH), BF16),
            pltpu.VMEM((2, PAIRS, LAG_LOCAL, BLOCK_CH, BLOCK_CH), BF16),
            pltpu.VMEM((BLOCKS, TILE, BLOCK_CH), BF16),
            pltpu.VMEM((BLOCKS, TILE, BLOCK_CH), BF16),
            dma((GROUPS,)), dma((5,)), dma((PAIRS,)), dma((PAIRS, GROUPS)),
            dma, dma, dma, dma, dma, dma, dma((4,)), dma((2, PAIRS)), dma((2, PAIRS)), dma, dma,
            dma, dma, dma, dma,
        ],
        compiler_params=pltpu.CompilerParams(
            collective_id=0, has_side_effects=True, vmem_limit_bytes=62 * 1024 * 1024
        ),
    )(records, jnp.asarray(fourier_rows()), jnp.asarray(lag_rows()), jnp.asarray(swap_rows()), offsets, sides)


def local(records, offsets, sides):
    first, second = correlations(records, offsets, sides)
    return first[None], second[None]


def solution(mesh):
    return jax.shard_map(
        local,
        mesh=mesh,
        in_specs=(P("blk", "pair", None), P(), P("blk", None)),
        out_specs=(P("blk", None, "pair", None, None), P("blk", None, "pair", None, None)),
        check_vma=False,
    )
```

```python
import functools
import math

import jax
import jax.numpy as jnp
import numpy as np
from jax import lax
from jax.experimental import pallas as pl
from jax.experimental.pallas import tpu as pltpu
from jax.sharding import PartitionSpec as P

BLOCK_CH = 128
BINS = 128
SAMPLES = 2048
FIRST_BIN = 4
LAGS = 32
SEGMENTS = 64
BLOCKS = 64
LAST_OFFSET = 15
PAIRS = 4
BIN_LOCAL = BINS // PAIRS
ROWS = 2 * BIN_LOCAL
LAG_LOCAL = LAGS // PAIRS
LAG_HALF = LAG_LOCAL // 2
LOCAL_BLOCKS = BLOCKS // PAIRS
GROUP = 2
GROUPS = LOCAL_BLOCKS // GROUP
BEHIND = 4
TILE = 16
BF16 = jnp.bfloat16
F32 = jnp.float32
MESH = pl.DeviceIdType.MESH


def fourier_rows():
    n = np.arange(SAMPLES, dtype=np.int64)
    k = FIRST_BIN + np.arange(BINS, dtype=np.int64)
    angles = 2.0 * math.pi / SAMPLES * (k[:, None] * n[None, :] % SAMPLES).astype(np.float64)
    taper = 0.5 - 0.5 * np.cos(2.0 * math.pi / SAMPLES * n.astype(np.float64))
    table = np.stack((taper * np.cos(angles), -taper * np.sin(angles)))
    table = table.reshape(2, PAIRS, BIN_LOCAL, SAMPLES).transpose(1, 0, 2, 3).reshape(2 * BINS, SAMPLES)
    high = table.astype(BF16)
    low = (table - high.astype(np.float64)).astype(BF16)
    return np.concatenate((high, low), axis=0)


def lag_rows():
    lag = np.arange(LAGS, dtype=np.int64) - LAGS // 2
    k = FIRST_BIN + np.arange(BINS, dtype=np.int64)
    angles = 2.0 * math.pi / SAMPLES * (lag[:, None] * k[None, :] % SAMPLES).astype(np.float64)
    table = np.stack((np.cos(angles), -np.sin(angles))) / math.sqrt(SEGMENTS * BINS)
    table = table.reshape(2, LAGS, PAIRS, BIN_LOCAL).transpose(2, 1, 0, 3).reshape(PAIRS, LAGS, ROWS)
    same = np.eye(TILE)
    spread = table[:, :, None, :, None] * same[None, None, :, None, :]
    return spread.reshape(PAIRS, LAGS * TILE, ROWS * TILE).astype(BF16)


def swap_rows():
    index = np.arange(TILE * TILE)
    table = np.zeros((TILE * TILE, TILE * TILE))
    table[index, (index % TILE) * TILE + index // TILE] = 1.0
    return table.astype(BF16)


def kernel(
    records, fourier, lagtab, swap, offsets_h, sides_h,
    first, second,
    rec_v, fourier_v, lagtab_v, swap_v, offsets, sides,
    shares, spectra, staged, own, far, near, own_t, far_t, cross, lagged, arrived, middle, onward, sums,
    load_sem, table_sem, ys, yr, own_s, own_r, near_s, near_r, far_s, far_r, here_sem, lag_s, lag_r, sec_s, sec_r,
    mid_s, mid_r, out_s, out_r,
):
    me = lax.axis_index("blk")
    q = lax.axis_index("pair")
    barrier = pltpu.get_barrier_semaphore()

    loads = []
    table_loads = [
        pltpu.make_async_copy(fourier, fourier_v, table_sem.at[0]),
        pltpu.make_async_copy(swap, swap_v, table_sem.at[1]),
        pltpu.make_async_copy(lagtab.at[q], lagtab_v, table_sem.at[2]),
        pltpu.make_async_copy(offsets_h, offsets, table_sem.at[3]),
        pltpu.make_async_copy(sides_h, sides, table_sem.at[4]),
    ]
    table_loads[0].start()
    width = GROUP * BLOCK_CH
    place = lax.rem(me // 2, GROUPS)

    def turn_of(g):
        ahead = (g % 2) * ((g + 1) // 2) + (1 - g % 2) * (GROUPS - g // 2)
        return lax.rem(place + ahead, GROUPS)

    for g in range(GROUPS):
        row = pl.multiple_of(turn_of(g) * width, width)
        copy = pltpu.make_async_copy(records.at[0, pl.ds(row, width)], rec_v.at[g], load_sem.at[g])
        copy.start()
        loads.append(copy)
    for copy in table_loads[1:]:
        copy.start()

    def greet(t, carry):
        pl.semaphore_signal(barrier, inc=1, device_id=(lax.rem(me + t, BLOCKS), q), device_id_type=MESH)
        return carry

    lax.fori_loop(1, BLOCKS, greet, 0)
    for t in range(1, PAIRS):
        pl.semaphore_signal(barrier, inc=1, device_id=(me, lax.rem(q + t, PAIRS)), device_id_type=MESH)

    def whiten(g):
        out = lax.dot_general(
            fourier_v[...], rec_v[g], (((1,), (1,)), ((), ())), preferred_element_type=F32
        )
        spectrum = (out[: 2 * BINS] + out[2 * BINS :]).reshape(PAIRS, 2, BIN_LOCAL, width)
        at = turn_of(g) * GROUP
        power = spectrum[:, 0] * spectrum[:, 0] + spectrum[:, 1] * spectrum[:, 1]
        for i in range(GROUP):
            lanes = slice(i * BLOCK_CH, (i + 1) * BLOCK_CH)
            level = jnp.sum(power[:, :, lanes], axis=-1, keepdims=True) * (1.0 / BLOCK_CH)
            scale = 1.0 / jnp.sqrt(level + 1e-05)
            white = (spectrum[:, :, :, lanes] * scale[:, None]).astype(BF16)
            shares[:, at + i] = white.reshape(PAIRS, ROWS, BLOCK_CH)
            spectra[q * LOCAL_BLOCKS + at + i] = shares[q, at + i]

    def send_block(source, target, b, send_sem, recv_sem):
        @pl.when(b != me)
        def _():
            pltpu.make_async_remote_copy(
                src_ref=source.at[b], dst_ref=target.at[me], send_sem=send_sem, recv_sem=recv_sem,
                device_id=(b, q), device_id_type=MESH,
            ).start()

    def send_group(g):
        at = turn_of(g) * GROUP
        for t in (2, 1, 3):
            peer = lax.rem(q + t, PAIRS)
            pltpu.make_async_remote_copy(
                src_ref=shares.at[peer, pl.ds(at, GROUP)],
                dst_ref=spectra.at[pl.ds(q * LOCAL_BLOCKS + at, GROUP)],
                send_sem=ys.at[t], recv_sem=yr.at[t, g],
                device_id=(me, peer), device_id_type=MESH,
            ).start()
        for i in range(GROUP):
            send_block(spectra, own, q * LOCAL_BLOCKS + at + i, own_s, own_r)

    def pass_on(g):
        at = turn_of(g) * GROUP
        two = spectra.at[pl.ds(0, GROUP)]
        for t in (1, 3, 2):
            pltpu.make_async_copy(two, two, yr.at[t, g]).wait()
            base = lax.rem(q + PAIRS - t, PAIRS) * LOCAL_BLOCKS
            for i in range(GROUP):
                send_block(spectra, own, base + at + i, own_s, own_r)

    table_loads[0].wait()
    loads[0].wait()
    whiten(0)
    pl.semaphore_wait(barrier, BLOCKS - 1 + PAIRS - 1)
    send_group(0)
    for g in range(1, GROUPS):
        loads[g].wait()

    def group_step(g, carry):
        whiten(g)
        send_group(g)
        return carry

    def late_step(g, carry):
        whiten(g)
        send_group(g)
        pass_on(g - BEHIND)
        return carry

    def pass_step(g, carry):
        pass_on(g)
        return carry

    lax.fori_loop(1, BEHIND, group_step, 0)
    lax.fori_loop(BEHIND, GROUPS, late_step, 0)
    lax.fori_loop(GROUPS - BEHIND, GROUPS, pass_step, 0)
    sixteen = spectra.at[pl.ds(0, LOCAL_BLOCKS)]
    own_here = pltpu.make_async_copy(spectra.at[me], own.at[me], here_sem.at[0])
    own_here.start()

    for copy in table_loads[1:]:
        copy.wait()
    offset = offsets[0]

    def alternate(t):
        ahead = (t % 2) * ((t + 1) // 2) + (1 - t % 2) * (BLOCKS - t // 2)
        return lax.rem(me + ahead, BLOCKS)

    def stage(b, carry):
        staged[b] = spectra[jnp.minimum(b + offset, BLOCKS - 1)]
        return carry

    lax.fori_loop(0, BLOCKS, stage, 0)
    near_here = pltpu.make_async_copy(staged.at[me], near.at[me], here_sem.at[1])
    near_here.start()

    def send_staged(t, carry):
        b = alternate(t)
        pltpu.make_async_remote_copy(
            src_ref=staged.at[b], dst_ref=near.at[me], send_sem=near_s, recv_sem=near_r,
            device_id=(b, q), device_id_type=MESH,
        ).start()
        return carry

    lax.fori_loop(1, BLOCKS, send_staged, 0)

    others = own.at[pl.ds(0, BLOCKS - 1)]
    own_here.wait()
    pltpu.make_async_copy(others, others, own_r).wait()
    down = me % LAST_OFFSET % 2 == 0
    has_lower = me >= LAST_OFFSET
    has_upper = me + LAST_OFFSET < BLOCKS
    lower = lax.rem(me + BLOCKS - LAST_OFFSET, BLOCKS)
    upper = lax.rem(me + LAST_OFFSET, BLOCKS)
    gives = (down & has_lower) | (~down & has_upper)
    works = (down & has_upper) | (~down & has_lower)
    own[SEGMENTS] = jnp.full((ROWS, BLOCK_CH), sides[0, 1].astype(F32), F32).astype(BF16)
    forward = pltpu.make_async_remote_copy(
        src_ref=own, dst_ref=far, send_sem=far_s, recv_sem=far_r,
        device_id=(jnp.where(down, lower, upper), q), device_id_type=MESH,
    )

    @pl.when(gives)
    def _():
        forward.start()

    def turn(source, target):
        for i in range(SEGMENTS // TILE):
            for j in range(0, ROWS // TILE, 2):
                segs = slice(i * TILE, (i + 1) * TILE)
                rows = [slice((j + n) * TILE, (j + n + 1) * TILE) for n in range(2)]
                tiles = [source[segs, row, :].reshape(TILE * TILE, BLOCK_CH) for row in rows]
                turned = jnp.dot(swap_v[...], jnp.concatenate(tiles, axis=1), preferred_element_type=F32).astype(BF16)
                for n in range(2):
                    lanes = slice(n * BLOCK_CH, (n + 1) * BLOCK_CH)
                    target[rows[n], segs, :] = turned[:, lanes].reshape(TILE, TILE, BLOCK_CH)

    turn(own, own_t)

    def correlate(k, swapped):
        straight = 1.0 - swapped

        def bin_step(f, carry):
            own_re, own_im = own_t[f], own_t[BIN_LOCAL + f]
            far_re, far_im = far_t[f], far_t[BIN_LOCAL + f]
            src_re = own_re * straight + far_re * swapped
            src_im = own_im * straight + far_im * swapped
            rec_re = far_re * straight + own_re * swapped
            rec_im = far_im * straight + own_im * swapped
            left = jnp.concatenate((src_re, src_im), axis=0)
            right = jnp.concatenate(
                (jnp.concatenate((rec_re, rec_im), axis=0), jnp.concatenate((rec_im, -rec_re), axis=0)), axis=1
            )
            out = lax.dot_general(left, right, (((0,), (0,)), ((), ())), preferred_element_type=F32)
            cross[f] = out[:, :BLOCK_CH].astype(BF16)
            cross[BIN_LOCAL + f] = out[:, BLOCK_CH:].astype(BF16)
            return carry

        lax.fori_loop(0, BIN_LOCAL, bin_step, 0, unroll=4)

        def lag_step(i, carry):
            c0 = pl.multiple_of(i * 2 * TILE, 2 * TILE)
            c1 = pl.multiple_of(i * 2 * TILE + TILE, TILE)
            cols = jnp.concatenate(
                (
                    cross[:, pl.ds(c0, TILE), :].reshape(ROWS * TILE, BLOCK_CH),
                    cross[:, pl.ds(c1, TILE), :].reshape(ROWS * TILE, BLOCK_CH),
                ),
                axis=1,
            )
            out = jnp.dot(lagtab_v[...], cols, preferred_element_type=F32).astype(BF16)
            lagged[k, :, pl.ds(c0, TILE), :] = out[:, :BLOCK_CH].reshape(LAGS, TILE, BLOCK_CH)
            lagged[k, :, pl.ds(c1, TILE), :] = out[:, BLOCK_CH:].reshape(LAGS, TILE, BLOCK_CH)
            return carry

        lax.fori_loop(0, BLOCK_CH // (2 * TILE), lag_step, 0, unroll=4)
        copies = []
        for h in range(2):
            for t in (2, 1, 3):
                peer = lax.rem(q + t, PAIRS)
                copy = pltpu.make_async_remote_copy(
                    src_ref=lagged.at[k, pl.ds(peer * LAG_LOCAL + h * LAG_HALF, LAG_HALF)],
                    dst_ref=arrived.at[k, t, pl.ds(h * LAG_HALF, LAG_HALF)],
                    send_sem=lag_s.at[k, t, h], recv_sem=lag_r.at[k, t, h],
                    device_id=(me, peer), device_id_type=MESH,
                )
                copy.start()
                copies.append(copy)
        return copies

    def lag_sums(k, h, copies, put):
        for copy in copies[h * (PAIRS - 1) : (h + 1) * (PAIRS - 1)]:
            copy.wait_recv()

        def lag_sum(l, carry):
            total = lagged[k, q * LAG_LOCAL + l].astype(F32)
            for t in range(1, PAIRS):
                total = total + arrived[k, t, l].astype(F32)
            put(l, total)
            return carry

        lax.fori_loop(h * LAG_HALF, (h + 1) * LAG_HALF, lag_sum, 0)

    near_here.wait()
    pltpu.make_async_copy(others, others, near_r).wait()
    turn(near, far_t)
    near_copies = correlate(0, jnp.full((SEGMENTS, BLOCK_CH), sides[0, 0].astype(F32), F32).astype(BF16))

    @pl.when(works)
    def _():
        forward.wait_recv()

    @pl.when(~works)
    def _():
        far[...] = jnp.zeros_like(far)

    turn(far, far_t)
    is_down = jnp.full((SEGMENTS, BLOCK_CH), jnp.where(down, 1, 0).astype(F32), F32).astype(BF16)
    last_copies = correlate(1, is_down * own[SEGMENTS] + (1.0 - is_down) * (1.0 - far[SEGMENTS]))

    def part(ref, m):
        n = m // 2
        lag = m % 2 * LAG_HALF + n // 8
        return ref.at[0, lag, pl.ds(pl.multiple_of(n % 8 * TILE, TILE), TILE)]

    keep = jnp.where(me + offset < BLOCKS, 1, 0).astype(F32)

    def put_near(l, total):
        first[0, l] = (total * keep).astype(BF16)

    for h in range(2):
        lag_sums(0, h, near_copies, put_near)

        def send_part(t, carry):
            ahead = (t % 2) * ((t + 1) // 2) + (1 - t % 2) * (BLOCKS // 2 - t // 2)
            m = lax.rem(me // 2 + ahead, BLOCKS // 2) * 2 + h

            @pl.when(m != me)
            def _():
                pltpu.make_async_remote_copy(
                    src_ref=part(first, m), dst_ref=middle.at[me], send_sem=mid_s, recv_sem=mid_r,
                    device_id=(m, q), device_id_type=MESH,
                ).start()

            return carry

        lax.fori_loop(0, BLOCKS // 2, send_part, 0)
    mid_here = pltpu.make_async_copy(part(first, me), middle.at[me], here_sem.at[2])
    mid_here.start()

    parts = middle.at[pl.ds(0, BLOCKS - 1)]
    mid_here.wait()
    pltpu.make_async_copy(parts, parts, mid_r).wait()

    def stage_part(j, carry):
        onward[j] = middle[lax.rem(j + BLOCKS - offset, BLOCKS)]
        return carry

    lax.fori_loop(0, BLOCKS, stage_part, 0)
    out_here = pltpu.make_async_copy(onward.at[me], part(second, me), here_sem.at[3])
    out_here.start()

    def send_onward(t, carry):
        j = alternate(t)
        pltpu.make_async_remote_copy(
            src_ref=onward.at[j], dst_ref=part(second, me), send_sem=out_s, recv_sem=out_r,
            device_id=(j, q), device_id_type=MESH,
        ).start()
        return carry

    lax.fori_loop(1, BLOCKS, send_onward, 0)
    def put_last(l, total):
        sums[l] = total.astype(BF16)

    for h in range(2):
        lag_sums(1, h, last_copies, put_last)

    def hand_over(target, device):
        return pltpu.make_async_remote_copy(
            src_ref=sums, dst_ref=target.at[1], send_sem=sec_s, recv_sem=sec_r,
            device_id=(device, q), device_id_type=MESH,
        )

    @pl.when(down & has_upper)
    def _():
        hand_over(second, upper).start()

    @pl.when(~down & has_lower)
    def _():
        hand_over(first, lower).start()

    @pl.when(down)
    def _():
        first[1] = sums[...]

    @pl.when(~down)
    def _():
        second[1] = sums[...]

    @pl.when(down & ~has_lower)
    def _():
        second[1] = jnp.zeros_like(sums)

    @pl.when(~down & ~has_upper)
    def _():
        first[1] = jnp.zeros_like(sums)

    out_here.wait()
    pltpu.make_async_copy(parts, parts, out_r).wait()

    @pl.when(gives)
    def _():
        pltpu.make_async_copy(sums, sums, sec_r).wait()

    for t in range(1, PAIRS):
        pltpu.make_async_copy(sixteen, sixteen, ys.at[t]).wait()
    pltpu.make_async_copy(others, others, own_s).wait()
    pltpu.make_async_copy(others, others, near_s).wait()

    @pl.when(gives)
    def _():
        forward.wait_send()

    for copy in last_copies + near_copies:
        copy.wait_send()

    @pl.when(works)
    def _():
        pltpu.make_async_copy(sums, sums, sec_s).wait()

    pltpu.make_async_copy(parts, parts, mid_s).wait()
    pltpu.make_async_copy(parts, parts, out_s).wait()


def correlations(records, offsets, sides):
    hbm = pl.BlockSpec(memory_space=pltpu.HBM)
    vmem = pl.BlockSpec(memory_space=pltpu.VMEM)
    whole = (BLOCKS, ROWS, BLOCK_CH)
    more = (SEGMENTS + 1, ROWS, BLOCK_CH)
    dma = pltpu.SemaphoreType.DMA
    return pl.pallas_call(
        kernel,
        name="correlations",
        out_shape=(
            jax.ShapeDtypeStruct((2, LAG_LOCAL, BLOCK_CH, BLOCK_CH), BF16),
            jax.ShapeDtypeStruct((2, LAG_LOCAL, BLOCK_CH, BLOCK_CH), BF16),
        ),
        in_specs=[hbm] * 6,
        out_specs=(vmem, vmem),
        scratch_shapes=[
            pltpu.VMEM((GROUPS, GROUP * BLOCK_CH, SAMPLES), BF16),
            pltpu.VMEM((4 * BINS, SAMPLES), BF16),
            pltpu.VMEM((LAGS * TILE, ROWS * TILE), BF16),
            pltpu.VMEM((TILE * TILE, TILE * TILE), BF16),
            pltpu.SMEM((2,), jnp.int32),
            pltpu.SMEM((1, 2), jnp.int32),
            pltpu.VMEM((PAIRS, LOCAL_BLOCKS, ROWS, BLOCK_CH), BF16),
            pltpu.VMEM(whole, BF16),
            pltpu.VMEM(whole, BF16),
            pltpu.VMEM(more, BF16),
            pltpu.VMEM(more, BF16),
            pltpu.VMEM(whole, BF16),
            pltpu.VMEM((ROWS, SEGMENTS, BLOCK_CH), BF16),
            pltpu.VMEM((ROWS, SEGMENTS, BLOCK_CH), BF16),
            pltpu.VMEM((ROWS, BLOCK_CH, BLOCK_CH), BF16),
            pltpu.VMEM((2, LAGS, BLOCK_CH, BLOCK_CH), BF16),
            pltpu.VMEM((2, PAIRS, LAG_LOCAL, BLOCK_CH, BLOCK_CH), BF16),
            pltpu.VMEM((BLOCKS, TILE, BLOCK_CH), BF16),
            pltpu.VMEM((BLOCKS, TILE, BLOCK_CH), BF16),
            pltpu.VMEM((LAG_LOCAL, BLOCK_CH, BLOCK_CH), BF16),
            dma((GROUPS,)), dma((5,)), dma((PAIRS,)), dma((PAIRS, GROUPS)),
            dma, dma, dma, dma, dma, dma, dma((4,)), dma((2, PAIRS, 2)), dma((2, PAIRS, 2)), dma, dma,
            dma, dma, dma, dma,
        ],
        compiler_params=pltpu.CompilerParams(
            collective_id=0, has_side_effects=True, vmem_limit_bytes=62 * 1024 * 1024
        ),
    )(records, jnp.asarray(fourier_rows()), jnp.asarray(lag_rows()), jnp.asarray(swap_rows()), offsets, sides)


def local(records, offsets, sides):
    first, second = correlations(records, offsets, sides)
    return first[None], second[None]


def solution(mesh):
    return jax.shard_map(
        local,
        mesh=mesh,
        in_specs=(P("blk", "pair", None), P(), P("blk", None)),
        out_specs=(P("blk", None, "pair", None, None), P("blk", None, "pair", None, None)),
        check_vma=False,
    )
```

```python
import functools
import math

import jax
import jax.numpy as jnp
import numpy as np
from jax import lax
from jax.experimental import pallas as pl
from jax.experimental.pallas import tpu as pltpu
from jax.sharding import PartitionSpec as P

BLOCK_CH = 128
BINS = 128
SAMPLES = 2048
FIRST_BIN = 4
LAGS = 32
SEGMENTS = 64
BLOCKS = 64
LAST_OFFSET = 15
PAIRS = 4
BIN_LOCAL = BINS // PAIRS
ROWS = 2 * BIN_LOCAL
LAG_LOCAL = LAGS // PAIRS
LAG_HALF = LAG_LOCAL // 2
LOCAL_BLOCKS = BLOCKS // PAIRS
GROUP = 2
GROUPS = LOCAL_BLOCKS // GROUP
BEHIND = 4
TILE = 16
BF16 = jnp.bfloat16
F32 = jnp.float32
MESH = pl.DeviceIdType.MESH


def fourier_rows():
    n = np.arange(SAMPLES, dtype=np.int64)
    k = FIRST_BIN + np.arange(BINS, dtype=np.int64)
    angles = 2.0 * math.pi / SAMPLES * (k[:, None] * n[None, :] % SAMPLES).astype(np.float64)
    taper = 0.5 - 0.5 * np.cos(2.0 * math.pi / SAMPLES * n.astype(np.float64))
    table = np.stack((taper * np.cos(angles), -taper * np.sin(angles)))
    table = table.reshape(2, PAIRS, BIN_LOCAL, SAMPLES).transpose(1, 0, 2, 3).reshape(2 * BINS, SAMPLES)
    high = table.astype(BF16)
    low = (table - high.astype(np.float64)).astype(BF16)
    return np.concatenate((high, low), axis=0)


def lag_rows():
    lag = np.arange(LAGS, dtype=np.int64) - LAGS // 2
    k = FIRST_BIN + np.arange(BINS, dtype=np.int64)
    angles = 2.0 * math.pi / SAMPLES * (lag[:, None] * k[None, :] % SAMPLES).astype(np.float64)
    table = np.stack((np.cos(angles), -np.sin(angles))) / math.sqrt(SEGMENTS * BINS)
    table = table.reshape(2, LAGS, PAIRS, BIN_LOCAL).transpose(2, 1, 0, 3).reshape(PAIRS, LAGS, ROWS)
    same = np.eye(TILE)
    spread = table[:, :, None, :, None] * same[None, None, :, None, :]
    return spread.reshape(PAIRS, LAGS * TILE, ROWS * TILE).astype(BF16)


def swap_rows():
    index = np.arange(TILE * TILE)
    table = np.zeros((TILE * TILE, TILE * TILE))
    table[index, (index % TILE) * TILE + index // TILE] = 1.0
    return table.astype(BF16)


def kernel(
    records, fourier, lagtab, swap, offsets_h, sides_h,
    first, second,
    rec_v, fourier_v, lagtab_v, swap_v, offsets, sides,
    shares, spectra, staged, own, far, near, own_t, far_t, cross, lagged, arrived, middle, onward, outgoing, sums,
    load_sem, table_sem, ys, yr, own_s, own_r, near_s, near_r, far_s, far_r, here_sem, lag_s, lag_r, sec_s, sec_r,
    mid_s, mid_r, out_s, out_r,
):
    me = lax.axis_index("blk")
    q = lax.axis_index("pair")
    barrier = pltpu.get_barrier_semaphore()

    loads = []
    table_loads = [
        pltpu.make_async_copy(fourier, fourier_v, table_sem.at[0]),
        pltpu.make_async_copy(swap, swap_v, table_sem.at[1]),
        pltpu.make_async_copy(lagtab.at[q], lagtab_v, table_sem.at[2]),
        pltpu.make_async_copy(offsets_h, offsets, table_sem.at[3]),
        pltpu.make_async_copy(sides_h, sides, table_sem.at[4]),
    ]
    table_loads[0].start()
    width = GROUP * BLOCK_CH
    place = lax.rem(me // 2, GROUPS)

    def turn_of(g):
        ahead = (g % 2) * ((g + 1) // 2) + (1 - g % 2) * (GROUPS - g // 2)
        return lax.rem(place + ahead, GROUPS)

    for g in range(GROUPS):
        row = pl.multiple_of(turn_of(g) * width, width)
        copy = pltpu.make_async_copy(records.at[0, pl.ds(row, width)], rec_v.at[g], load_sem.at[g])
        copy.start()
        loads.append(copy)
    for copy in table_loads[1:]:
        copy.start()

    def wrapped(value, count):
        value = jnp.where(value >= count, value - count, value)
        return jnp.where(value < 0, value + count, value)

    def both_ways(here, count, send):
        def step(t, carry):
            send(wrapped(here + count // 2 - t, count))
            send(wrapped(here - count // 2 + t, count))
            return carry

        send(wrapped(here + count // 2, count))
        lax.fori_loop(1, count // 2, step, 0)

    def greet(b):
        pl.semaphore_signal(barrier, inc=1, device_id=(b, q), device_id_type=MESH)

    both_ways(me, BLOCKS, greet)
    for t in range(1, PAIRS):
        pl.semaphore_signal(barrier, inc=1, device_id=(me, lax.rem(q + t, PAIRS)), device_id_type=MESH)

    def whiten(g):
        out = lax.dot_general(
            fourier_v[...], rec_v[g], (((1,), (1,)), ((), ())), preferred_element_type=F32
        )
        spectrum = (out[: 2 * BINS] + out[2 * BINS :]).reshape(PAIRS, 2, BIN_LOCAL, width)
        at = turn_of(g) * GROUP
        power = spectrum[:, 0] * spectrum[:, 0] + spectrum[:, 1] * spectrum[:, 1]
        for i in range(GROUP):
            lanes = slice(i * BLOCK_CH, (i + 1) * BLOCK_CH)
            level = jnp.sum(power[:, :, lanes], axis=-1, keepdims=True) * (1.0 / BLOCK_CH)
            scale = 1.0 / jnp.sqrt(level + 1e-05)
            white = (spectrum[:, :, :, lanes] * scale[:, None]).astype(BF16)
            shares[:, at + i] = white.reshape(PAIRS, ROWS, BLOCK_CH)
            spectra[q * LOCAL_BLOCKS + at + i] = shares[q, at + i]

    def send_block(source, target, b, send_sem, recv_sem):
        @pl.when(b != me)
        def _():
            pltpu.make_async_remote_copy(
                src_ref=source.at[b], dst_ref=target.at[me], send_sem=send_sem, recv_sem=recv_sem,
                device_id=(b, q), device_id_type=MESH,
            ).start()

    def send_group(g):
        at = turn_of(g) * GROUP
        for t in (2, 1, 3):
            peer = lax.rem(q + t, PAIRS)
            pltpu.make_async_remote_copy(
                src_ref=shares.at[peer, pl.ds(at, GROUP)],
                dst_ref=spectra.at[pl.ds(q * LOCAL_BLOCKS + at, GROUP)],
                send_sem=ys.at[t], recv_sem=yr.at[t, g],
                device_id=(me, peer), device_id_type=MESH,
            ).start()
        for i in range(GROUP):
            send_block(spectra, own, q * LOCAL_BLOCKS + at + i, own_s, own_r)

    def pass_on(g):
        at = turn_of(g) * GROUP
        two = spectra.at[pl.ds(0, GROUP)]
        for t in (1, 3, 2):
            pltpu.make_async_copy(two, two, yr.at[t, g]).wait()
            base = lax.rem(q + PAIRS - t, PAIRS) * LOCAL_BLOCKS
            for i in range(GROUP):
                send_block(spectra, own, base + at + i, own_s, own_r)

    table_loads[0].wait()
    loads[0].wait()
    whiten(0)
    pl.semaphore_wait(barrier, BLOCKS - 1 + PAIRS - 1)
    send_group(0)
    for g in range(1, GROUPS):
        loads[g].wait()

    def group_step(g, carry):
        whiten(g)
        send_group(g)
        return carry

    def late_step(g, carry):
        whiten(g)
        send_group(g)
        pass_on(g - BEHIND)
        return carry

    def pass_step(g, carry):
        pass_on(g)
        return carry

    lax.fori_loop(1, BEHIND, group_step, 0)
    lax.fori_loop(BEHIND, GROUPS, late_step, 0)
    lax.fori_loop(GROUPS - BEHIND, GROUPS, pass_step, 0)
    sixteen = spectra.at[pl.ds(0, LOCAL_BLOCKS)]
    own_here = pltpu.make_async_copy(spectra.at[me], own.at[me], here_sem.at[0])
    own_here.start()

    for copy in table_loads[1:]:
        copy.wait()
    offset = offsets[0]

    def stage(b, carry):
        staged[b] = spectra[jnp.minimum(b + offset, BLOCKS - 1)]
        return carry

    lax.fori_loop(0, BLOCKS, stage, 0)
    near_here = pltpu.make_async_copy(staged.at[me], near.at[me], here_sem.at[1])
    near_here.start()

    def send_staged(b):
        pltpu.make_async_remote_copy(
            src_ref=staged.at[b], dst_ref=near.at[me], send_sem=near_s, recv_sem=near_r,
            device_id=(b, q), device_id_type=MESH,
        ).start()

    both_ways(me, BLOCKS, send_staged)

    others = own.at[pl.ds(0, BLOCKS - 1)]
    own_here.wait()
    pltpu.make_async_copy(others, others, own_r).wait()
    down = me % LAST_OFFSET % 2 == 0
    has_lower = me >= LAST_OFFSET
    has_upper = me + LAST_OFFSET < BLOCKS
    lower = lax.rem(me + BLOCKS - LAST_OFFSET, BLOCKS)
    upper = lax.rem(me + LAST_OFFSET, BLOCKS)
    gives = (down & has_lower) | (~down & has_upper)
    works = (down & has_upper) | (~down & has_lower)
    own[SEGMENTS] = jnp.full((ROWS, BLOCK_CH), sides[0, 1].astype(F32), F32).astype(BF16)
    receiver = jnp.where(down, lower, upper)

    def forward(start, count):
        piece = pl.ds(start, count)
        return pltpu.make_async_remote_copy(
            src_ref=own.at[piece], dst_ref=far.at[piece], send_sem=far_s, recv_sem=far_r,
            device_id=(receiver, q), device_id_type=MESH,
        )

    @pl.when(gives)
    def _():
        for start, count in ((0, 16), (16, 16), (32, 16), (48, 17)):
            forward(start, count).start()

    def turn(source, target):
        for i in range(SEGMENTS // TILE):
            for j in range(0, ROWS // TILE, 2):
                segs = slice(i * TILE, (i + 1) * TILE)
                rows = [slice((j + n) * TILE, (j + n + 1) * TILE) for n in range(2)]
                tiles = [source[segs, row, :].reshape(TILE * TILE, BLOCK_CH) for row in rows]
                turned = jnp.dot(swap_v[...], jnp.concatenate(tiles, axis=1), preferred_element_type=F32).astype(BF16)
                for n in range(2):
                    lanes = slice(n * BLOCK_CH, (n + 1) * BLOCK_CH)
                    target[rows[n], segs, :] = turned[:, lanes].reshape(TILE, TILE, BLOCK_CH)

    turn(own, own_t)

    def correlate(k, swapped):
        straight = 1.0 - swapped

        def bin_step(f, carry):
            own_re, own_im = own_t[f], own_t[BIN_LOCAL + f]
            far_re, far_im = far_t[f], far_t[BIN_LOCAL + f]
            src_re = own_re * straight + far_re * swapped
            src_im = own_im * straight + far_im * swapped
            rec_re = far_re * straight + own_re * swapped
            rec_im = far_im * straight + own_im * swapped
            left = jnp.concatenate((src_re, src_im), axis=0)
            right = jnp.concatenate(
                (jnp.concatenate((rec_re, rec_im), axis=0), jnp.concatenate((rec_im, -rec_re), axis=0)), axis=1
            )
            out = lax.dot_general(left, right, (((0,), (0,)), ((), ())), preferred_element_type=F32)
            cross[f] = out[:, :BLOCK_CH].astype(BF16)
            cross[BIN_LOCAL + f] = out[:, BLOCK_CH:].astype(BF16)
            return carry

        lax.fori_loop(0, BIN_LOCAL, bin_step, 0, unroll=4)

        def lag_step(i, carry):
            c0 = pl.multiple_of(i * 2 * TILE, 2 * TILE)
            c1 = pl.multiple_of(i * 2 * TILE + TILE, TILE)
            cols = jnp.concatenate(
                (
                    cross[:, pl.ds(c0, TILE), :].reshape(ROWS * TILE, BLOCK_CH),
                    cross[:, pl.ds(c1, TILE), :].reshape(ROWS * TILE, BLOCK_CH),
                ),
                axis=1,
            )
            out = jnp.dot(lagtab_v[...], cols, preferred_element_type=F32).astype(BF16)
            lagged[k, :, pl.ds(c0, TILE), :] = out[:, :BLOCK_CH].reshape(LAGS, TILE, BLOCK_CH)
            lagged[k, :, pl.ds(c1, TILE), :] = out[:, BLOCK_CH:].reshape(LAGS, TILE, BLOCK_CH)
            return carry

        lax.fori_loop(0, BLOCK_CH // (2 * TILE), lag_step, 0, unroll=4)
        copies = []
        for h in range(2):
            for t in (2, 1, 3):
                peer = lax.rem(q + t, PAIRS)
                copy = pltpu.make_async_remote_copy(
                    src_ref=lagged.at[k, pl.ds(peer * LAG_LOCAL + h * LAG_HALF, LAG_HALF)],
                    dst_ref=arrived.at[k, t, pl.ds(h * LAG_HALF, LAG_HALF)],
                    send_sem=lag_s.at[k, t, h], recv_sem=lag_r.at[k, t, h],
                    device_id=(me, peer), device_id_type=MESH,
                )
                copy.start()
                copies.append(copy)
        return copies

    def lag_sums(k, h, copies, put):
        for copy in copies[h * (PAIRS - 1) : (h + 1) * (PAIRS - 1)]:
            copy.wait_recv()

        for l in range(h * LAG_HALF, (h + 1) * LAG_HALF):
            total = lagged[k, q * LAG_LOCAL + l].astype(F32)
            for t in range(1, PAIRS):
                total = total + arrived[k, t, l].astype(F32)
            put(l, total)

    near_here.wait()
    pltpu.make_async_copy(others, others, near_r).wait()
    turn(near, far_t)
    near_copies = correlate(0, jnp.full((SEGMENTS, BLOCK_CH), sides[0, 0].astype(F32), F32).astype(BF16))

    @pl.when(works)
    def _():
        pltpu.make_async_copy(far, far, far_r).wait()

    @pl.when(~works)
    def _():
        far[...] = jnp.zeros_like(far)

    turn(far, far_t)
    is_down = jnp.full((SEGMENTS, BLOCK_CH), jnp.where(down, 1, 0).astype(F32), F32).astype(BF16)
    last_copies = correlate(1, is_down * own[SEGMENTS] + (1.0 - is_down) * (1.0 - far[SEGMENTS]))

    keep = jnp.where(me + offset < BLOCKS, 1, 0).astype(F32)

    chip = me // 2

    def put_near(l, total):
        value = (total * keep).astype(BF16)
        first[0, l] = value
        for r in range(BLOCK_CH // TILE):
            m = 2 * (l % LAG_HALF * (BLOCK_CH // TILE) + r) + l // LAG_HALF
            outgoing[m] = value[r * TILE : (r + 1) * TILE]

    for h in range(2):
        lag_sums(0, h, near_copies, put_near)

        def send_part(m):
            pltpu.make_async_remote_copy(
                src_ref=outgoing.at[m], dst_ref=middle.at[me], send_sem=mid_s, recv_sem=mid_r,
                device_id=(m, q), device_id_type=MESH,
            ).start()

        @pl.when(2 * chip + h != me)
        def _():
            send_part(2 * chip + h)

        both_ways(chip, BLOCKS // 2, lambda n: send_part(2 * n + h))
    mid_here = pltpu.make_async_copy(outgoing.at[me], middle.at[me], here_sem.at[2])
    mid_here.start()

    parts = middle.at[pl.ds(0, BLOCKS - 1)]
    mid_here.wait()
    pltpu.make_async_copy(parts, parts, mid_r).wait()

    def stage_part(j, carry):
        onward[j] = middle[wrapped(j - offset, BLOCKS)]
        return carry

    lax.fori_loop(0, BLOCKS, stage_part, 0)
    spot = second.at[
        0, me % 2 * LAG_HALF + me // 2 // 8, pl.ds(pl.multiple_of(me // 2 % 8 * TILE, TILE), TILE)
    ]
    out_here = pltpu.make_async_copy(onward.at[me], spot, here_sem.at[3])
    out_here.start()

    def send_onward(j):
        pltpu.make_async_remote_copy(
            src_ref=onward.at[j], dst_ref=spot, send_sem=out_s, recv_sem=out_r,
            device_id=(j, q), device_id_type=MESH,
        ).start()

    both_ways(me, BLOCKS, send_onward)
    def put_last(l, total):
        sums[l] = total.astype(BF16)

    def hand_over(target, device, h):
        half = pl.ds(h * LAG_HALF, LAG_HALF)
        return pltpu.make_async_remote_copy(
            src_ref=sums.at[half], dst_ref=target.at[1, half], send_sem=sec_s, recv_sem=sec_r,
            device_id=(device, q), device_id_type=MESH,
        )

    for h in range(2):
        lag_sums(1, h, last_copies, put_last)

        @pl.when(down & has_upper)
        def _():
            hand_over(second, upper, h).start()

        @pl.when(~down & has_lower)
        def _():
            hand_over(first, lower, h).start()

    @pl.when(down)
    def _():
        first[1] = sums[...]

    @pl.when(~down)
    def _():
        second[1] = sums[...]

    @pl.when(down & ~has_lower)
    def _():
        second[1] = jnp.zeros_like(sums)

    @pl.when(~down & ~has_upper)
    def _():
        first[1] = jnp.zeros_like(sums)

    out_here.wait()
    pltpu.make_async_copy(parts, parts, out_r).wait()

    @pl.when(gives)
    def _():
        pltpu.make_async_copy(sums, sums, sec_r).wait()

    for t in range(1, PAIRS):
        pltpu.make_async_copy(sixteen, sixteen, ys.at[t]).wait()
    pltpu.make_async_copy(others, others, own_s).wait()
    pltpu.make_async_copy(others, others, near_s).wait()

    @pl.when(gives)
    def _():
        pltpu.make_async_copy(own, own, far_s).wait()

    for copy in last_copies + near_copies:
        copy.wait_send()

    @pl.when(works)
    def _():
        pltpu.make_async_copy(sums, sums, sec_s).wait()

    pltpu.make_async_copy(parts, parts, mid_s).wait()
    pltpu.make_async_copy(parts, parts, out_s).wait()


def correlations(records, offsets, sides):
    hbm = pl.BlockSpec(memory_space=pltpu.HBM)
    vmem = pl.BlockSpec(memory_space=pltpu.VMEM)
    whole = (BLOCKS, ROWS, BLOCK_CH)
    more = (SEGMENTS + 1, ROWS, BLOCK_CH)
    dma = pltpu.SemaphoreType.DMA
    return pl.pallas_call(
        kernel,
        name="correlations",
        out_shape=(
            jax.ShapeDtypeStruct((2, LAG_LOCAL, BLOCK_CH, BLOCK_CH), BF16),
            jax.ShapeDtypeStruct((2, LAG_LOCAL, BLOCK_CH, BLOCK_CH), BF16),
        ),
        in_specs=[hbm] * 6,
        out_specs=(vmem, vmem),
        scratch_shapes=[
            pltpu.VMEM((GROUPS, GROUP * BLOCK_CH, SAMPLES), BF16),
            pltpu.VMEM((4 * BINS, SAMPLES), BF16),
            pltpu.VMEM((LAGS * TILE, ROWS * TILE), BF16),
            pltpu.VMEM((TILE * TILE, TILE * TILE), BF16),
            pltpu.SMEM((2,), jnp.int32),
            pltpu.SMEM((1, 2), jnp.int32),
            pltpu.VMEM((PAIRS, LOCAL_BLOCKS, ROWS, BLOCK_CH), BF16),
            pltpu.VMEM(whole, BF16),
            pltpu.VMEM(whole, BF16),
            pltpu.VMEM(more, BF16),
            pltpu.VMEM(more, BF16),
            pltpu.VMEM(whole, BF16),
            pltpu.VMEM((ROWS, SEGMENTS, BLOCK_CH), BF16),
            pltpu.VMEM((ROWS, SEGMENTS, BLOCK_CH), BF16),
            pltpu.VMEM((ROWS, BLOCK_CH, BLOCK_CH), BF16),
            pltpu.VMEM((2, LAGS, BLOCK_CH, BLOCK_CH), BF16),
            pltpu.VMEM((2, PAIRS, LAG_LOCAL, BLOCK_CH, BLOCK_CH), BF16),
            pltpu.VMEM((BLOCKS, TILE, BLOCK_CH), BF16),
            pltpu.VMEM((BLOCKS, TILE, BLOCK_CH), BF16),
            pltpu.VMEM((BLOCKS, TILE, BLOCK_CH), BF16),
            pltpu.VMEM((LAG_LOCAL, BLOCK_CH, BLOCK_CH), BF16),
            dma((GROUPS,)), dma((5,)), dma((PAIRS,)), dma((PAIRS, GROUPS)),
            dma, dma, dma, dma, dma, dma, dma((4,)), dma((2, PAIRS, 2)), dma((2, PAIRS, 2)), dma, dma,
            dma, dma, dma, dma,
        ],
        compiler_params=pltpu.CompilerParams(
            collective_id=0, has_side_effects=True, vmem_limit_bytes=62 * 1024 * 1024
        ),
    )(records, jnp.asarray(fourier_rows()), jnp.asarray(lag_rows()), jnp.asarray(swap_rows()), offsets, sides)


def local(records, offsets, sides):
    first, second = correlations(records, offsets, sides)
    return first[None], second[None]


def solution(mesh):
    return jax.shard_map(
        local,
        mesh=mesh,
        in_specs=(P("blk", "pair", None), P(), P("blk", None)),
        out_specs=(P("blk", None, "pair", None, None), P("blk", None, "pair", None, None)),
        check_vma=False,
    )
```

```python
import functools
import math

import jax
import jax.numpy as jnp
import numpy as np
from jax import lax
from jax.experimental import pallas as pl
from jax.experimental.pallas import tpu as pltpu
from jax.sharding import PartitionSpec as P

BLOCK_CH = 128
BINS = 128
SAMPLES = 2048
FIRST_BIN = 4
LAGS = 32
SEGMENTS = 64
BLOCKS = 64
LAST_OFFSET = 15
PAIRS = 4
BIN_LOCAL = BINS // PAIRS
ROWS = 2 * BIN_LOCAL
LAG_LOCAL = LAGS // PAIRS
LAG_HALF = LAG_LOCAL // 2
LOCAL_BLOCKS = BLOCKS // PAIRS
GROUP = 2
GROUPS = LOCAL_BLOCKS // GROUP
BEHIND = 4
TILE = 16
BF16 = jnp.bfloat16
F32 = jnp.float32
MESH = pl.DeviceIdType.MESH


def fourier_rows():
    n = np.arange(SAMPLES, dtype=np.int64)
    k = FIRST_BIN + np.arange(BINS, dtype=np.int64)
    angles = 2.0 * math.pi / SAMPLES * (k[:, None] * n[None, :] % SAMPLES).astype(np.float64)
    taper = 0.5 - 0.5 * np.cos(2.0 * math.pi / SAMPLES * n.astype(np.float64))
    table = np.stack((taper * np.cos(angles), -taper * np.sin(angles)))
    table = table.reshape(2, PAIRS, BIN_LOCAL, SAMPLES).transpose(1, 0, 2, 3).reshape(2 * BINS, SAMPLES)
    high = table.astype(BF16)
    low = (table - high.astype(np.float64)).astype(BF16)
    return np.concatenate((high, low), axis=0)


def lag_rows():
    lag = np.arange(LAGS, dtype=np.int64) - LAGS // 2
    k = FIRST_BIN + np.arange(BINS, dtype=np.int64)
    angles = 2.0 * math.pi / SAMPLES * (lag[:, None] * k[None, :] % SAMPLES).astype(np.float64)
    table = np.stack((np.cos(angles), -np.sin(angles))) / math.sqrt(SEGMENTS * BINS)
    table = table.reshape(2, LAGS, PAIRS, BIN_LOCAL).transpose(2, 1, 0, 3).reshape(PAIRS, LAGS, ROWS)
    same = np.eye(TILE)
    spread = table[:, :, None, :, None] * same[None, None, :, None, :]
    return spread.reshape(PAIRS, LAGS * TILE, ROWS * TILE).astype(BF16)


def swap_rows():
    index = np.arange(TILE * TILE)
    table = np.zeros((TILE * TILE, TILE * TILE))
    table[index, (index % TILE) * TILE + index // TILE] = 1.0
    return table.astype(BF16)


def kernel(
    records, fourier, lagtab, swap, offsets_h, sides_h,
    first, second,
    rec_v, fourier_v, lagtab_v, swap_v, offsets, sides,
    shares, spectra, staged, own, far, near, own_t, far_t, cross, lagged, arrived, middle, onward, outgoing, sums,
    load_sem, table_sem, ys, yr, own_s, own_r, near_s, near_r, far_s, far_r, here_sem, lag_s, lag_r, sec_s, sec_r,
    mid_s, mid_r, out_s, out_r,
):
    me = lax.axis_index("blk")
    q = lax.axis_index("pair")
    barrier = pltpu.get_barrier_semaphore()

    loads = []
    table_loads = [
        pltpu.make_async_copy(fourier, fourier_v, table_sem.at[0]),
        pltpu.make_async_copy(swap, swap_v, table_sem.at[1]),
        pltpu.make_async_copy(lagtab.at[q], lagtab_v, table_sem.at[2]),
        pltpu.make_async_copy(offsets_h, offsets, table_sem.at[3]),
        pltpu.make_async_copy(sides_h, sides, table_sem.at[4]),
    ]
    table_loads[0].start()
    width = GROUP * BLOCK_CH
    place = lax.rem(me // 2, GROUPS)

    def turn_of(g):
        ahead = (g % 2) * ((g + 1) // 2) + (1 - g % 2) * (GROUPS - g // 2)
        return lax.rem(place + GROUPS // 2 + ahead, GROUPS)

    for g in range(GROUPS):
        row = pl.multiple_of(turn_of(g) * width, width)
        copy = pltpu.make_async_copy(records.at[0, pl.ds(row, width)], rec_v.at[g], load_sem.at[g])
        copy.start()
        loads.append(copy)
    for copy in table_loads[1:]:
        copy.start()

    def wrapped(value, count):
        value = jnp.where(value >= count, value - count, value)
        return jnp.where(value < 0, value + count, value)

    def both_ways(here, count, send):
        def step(t, carry):
            send(wrapped(here + count // 2 - t, count))
            send(wrapped(here - count // 2 + t, count))
            return carry

        send(wrapped(here + count // 2, count))
        lax.fori_loop(1, count // 2, step, 0)

    def greet(b):
        pl.semaphore_signal(barrier, inc=1, device_id=(b, q), device_id_type=MESH)

    both_ways(me, BLOCKS, greet)
    for t in range(1, PAIRS):
        pl.semaphore_signal(barrier, inc=1, device_id=(me, lax.rem(q + t, PAIRS)), device_id_type=MESH)

    def whiten(g):
        out = lax.dot_general(
            fourier_v[...], rec_v[g], (((1,), (1,)), ((), ())), preferred_element_type=F32
        )
        spectrum = (out[: 2 * BINS] + out[2 * BINS :]).reshape(PAIRS, 2, BIN_LOCAL, width)
        at = turn_of(g) * GROUP
        power = spectrum[:, 0] * spectrum[:, 0] + spectrum[:, 1] * spectrum[:, 1]
        for i in range(GROUP):
            lanes = slice(i * BLOCK_CH, (i + 1) * BLOCK_CH)
            level = jnp.sum(power[:, :, lanes], axis=-1, keepdims=True) * (1.0 / BLOCK_CH)
            scale = 1.0 / jnp.sqrt(level + 1e-05)
            white = (spectrum[:, :, :, lanes] * scale[:, None]).astype(BF16)
            shares[:, at + i] = white.reshape(PAIRS, ROWS, BLOCK_CH)
            spectra[q * LOCAL_BLOCKS + at + i] = shares[q, at + i]

    def send_block(source, target, b, send_sem, recv_sem):
        @pl.when(b != me)
        def _():
            pltpu.make_async_remote_copy(
                src_ref=source.at[b], dst_ref=target.at[me], send_sem=send_sem, recv_sem=recv_sem,
                device_id=(b, q), device_id_type=MESH,
            ).start()

    def send_group(g):
        at = turn_of(g) * GROUP
        for t in (2, 1, 3):
            peer = lax.rem(q + t, PAIRS)
            pltpu.make_async_remote_copy(
                src_ref=shares.at[peer, pl.ds(at, GROUP)],
                dst_ref=spectra.at[pl.ds(q * LOCAL_BLOCKS + at, GROUP)],
                send_sem=ys.at[t], recv_sem=yr.at[t, g],
                device_id=(me, peer), device_id_type=MESH,
            ).start()
        for i in range(GROUP):
            send_block(spectra, own, q * LOCAL_BLOCKS + at + i, own_s, own_r)

    def pass_on(g):
        at = turn_of(g) * GROUP
        two = spectra.at[pl.ds(0, GROUP)]
        for t in (1, 3, 2):
            pltpu.make_async_copy(two, two, yr.at[t, g]).wait()
            base = lax.rem(q + PAIRS - t, PAIRS) * LOCAL_BLOCKS
            for i in range(GROUP):
                send_block(spectra, own, base + at + i, own_s, own_r)

    table_loads[0].wait()
    loads[0].wait()
    whiten(0)
    pl.semaphore_wait(barrier, BLOCKS - 1 + PAIRS - 1)
    send_group(0)
    for g in range(1, GROUPS):
        loads[g].wait()

    def group_step(g, carry):
        whiten(g)
        send_group(g)
        return carry

    def late_step(g, carry):
        whiten(g)
        send_group(g)
        pass_on(g - BEHIND)
        return carry

    def pass_step(g, carry):
        pass_on(g)
        return carry

    lax.fori_loop(1, BEHIND, group_step, 0)
    lax.fori_loop(BEHIND, GROUPS, late_step, 0)
    lax.fori_loop(GROUPS - BEHIND, GROUPS, pass_step, 0)
    sixteen = spectra.at[pl.ds(0, LOCAL_BLOCKS)]
    own_here = pltpu.make_async_copy(spectra.at[me], own.at[me], here_sem.at[0])
    own_here.start()

    for copy in table_loads[1:]:
        copy.wait()
    offset = offsets[0]

    def stage(b, carry):
        staged[b] = spectra[jnp.minimum(b + offset, BLOCKS - 1)]
        return carry

    lax.fori_loop(0, BLOCKS, stage, 0)
    near_here = pltpu.make_async_copy(staged.at[me], near.at[me], here_sem.at[1])
    near_here.start()

    def send_staged(b):
        pltpu.make_async_remote_copy(
            src_ref=staged.at[b], dst_ref=near.at[me], send_sem=near_s, recv_sem=near_r,
            device_id=(b, q), device_id_type=MESH,
        ).start()

    both_ways(me, BLOCKS, send_staged)

    others = own.at[pl.ds(0, BLOCKS - 1)]
    own_here.wait()
    pltpu.make_async_copy(others, others, own_r).wait()
    down = me % LAST_OFFSET % 2 == 0
    has_lower = me >= LAST_OFFSET
    has_upper = me + LAST_OFFSET < BLOCKS
    lower = lax.rem(me + BLOCKS - LAST_OFFSET, BLOCKS)
    upper = lax.rem(me + LAST_OFFSET, BLOCKS)
    gives = (down & has_lower) | (~down & has_upper)
    works = (down & has_upper) | (~down & has_lower)
    own[SEGMENTS] = jnp.full((ROWS, BLOCK_CH), sides[0, 1].astype(F32), F32).astype(BF16)
    receiver = jnp.where(down, lower, upper)

    def forward(start, count):
        piece = pl.ds(start, count)
        return pltpu.make_async_remote_copy(
            src_ref=own.at[piece], dst_ref=far.at[piece], send_sem=far_s, recv_sem=far_r,
            device_id=(receiver, q), device_id_type=MESH,
        )

    @pl.when(gives)
    def _():
        for start, count in ((0, 16), (16, 16), (32, 16), (48, 17)):
            forward(start, count).start()

    def turn(source, target):
        for i in range(SEGMENTS // TILE):
            for j in range(0, ROWS // TILE, 2):
                segs = slice(i * TILE, (i + 1) * TILE)
                rows = [slice((j + n) * TILE, (j + n + 1) * TILE) for n in range(2)]
                tiles = [source[segs, row, :].reshape(TILE * TILE, BLOCK_CH) for row in rows]
                turned = jnp.dot(swap_v[...], jnp.concatenate(tiles, axis=1), preferred_element_type=F32).astype(BF16)
                for n in range(2):
                    lanes = slice(n * BLOCK_CH, (n + 1) * BLOCK_CH)
                    target[rows[n], segs, :] = turned[:, lanes].reshape(TILE, TILE, BLOCK_CH)

    turn(own, own_t)

    def correlate(k, swapped):
        straight = 1.0 - swapped

        def bin_step(f, carry):
            own_re, own_im = own_t[f], own_t[BIN_LOCAL + f]
            far_re, far_im = far_t[f], far_t[BIN_LOCAL + f]
            src_re = own_re * straight + far_re * swapped
            src_im = own_im * straight + far_im * swapped
            rec_re = far_re * straight + own_re * swapped
            rec_im = far_im * straight + own_im * swapped
            left = jnp.concatenate((src_re, src_im), axis=0)
            right = jnp.concatenate(
                (jnp.concatenate((rec_re, rec_im), axis=0), jnp.concatenate((rec_im, -rec_re), axis=0)), axis=1
            )
            out = lax.dot_general(left, right, (((0,), (0,)), ((), ())), preferred_element_type=F32)
            cross[f] = out[:, :BLOCK_CH].astype(BF16)
            cross[BIN_LOCAL + f] = out[:, BLOCK_CH:].astype(BF16)
            return carry

        lax.fori_loop(0, BIN_LOCAL, bin_step, 0, unroll=4)

        def lag_step(i, carry):
            c0 = pl.multiple_of(i * 2 * TILE, 2 * TILE)
            c1 = pl.multiple_of(i * 2 * TILE + TILE, TILE)
            cols = jnp.concatenate(
                (
                    cross[:, pl.ds(c0, TILE), :].reshape(ROWS * TILE, BLOCK_CH),
                    cross[:, pl.ds(c1, TILE), :].reshape(ROWS * TILE, BLOCK_CH),
                ),
                axis=1,
            )
            out = jnp.dot(lagtab_v[...], cols, preferred_element_type=F32).astype(BF16)
            lagged[k, :, pl.ds(c0, TILE), :] = out[:, :BLOCK_CH].reshape(LAGS, TILE, BLOCK_CH)
            lagged[k, :, pl.ds(c1, TILE), :] = out[:, BLOCK_CH:].reshape(LAGS, TILE, BLOCK_CH)
            return carry

        lax.fori_loop(0, BLOCK_CH // (2 * TILE), lag_step, 0, unroll=4)
        copies = []
        for h in range(2):
            for t in (2, 1, 3):
                peer = lax.rem(q + t, PAIRS)
                copy = pltpu.make_async_remote_copy(
                    src_ref=lagged.at[k, pl.ds(peer * LAG_LOCAL + h * LAG_HALF, LAG_HALF)],
                    dst_ref=arrived.at[k, t, pl.ds(h * LAG_HALF, LAG_HALF)],
                    send_sem=lag_s.at[k, t, h], recv_sem=lag_r.at[k, t, h],
                    device_id=(me, peer), device_id_type=MESH,
                )
                copy.start()
                copies.append(copy)
        return copies

    def lag_sums(k, h, copies, put):
        for copy in copies[h * (PAIRS - 1) : (h + 1) * (PAIRS - 1)]:
            copy.wait_recv()

        for l in range(h * LAG_HALF, (h + 1) * LAG_HALF):
            total = lagged[k, q * LAG_LOCAL + l].astype(F32)
            for t in range(1, PAIRS):
                total = total + arrived[k, t, l].astype(F32)
            put(l, total)

    near_here.wait()
    pltpu.make_async_copy(others, others, near_r).wait()
    turn(near, far_t)
    near_copies = correlate(0, jnp.full((SEGMENTS, BLOCK_CH), sides[0, 0].astype(F32), F32).astype(BF16))

    @pl.when(works)
    def _():
        pltpu.make_async_copy(far, far, far_r).wait()

    @pl.when(~works)
    def _():
        far[...] = jnp.zeros_like(far)

    turn(far, far_t)
    is_down = jnp.full((SEGMENTS, BLOCK_CH), jnp.where(down, 1, 0).astype(F32), F32).astype(BF16)
    last_copies = correlate(1, is_down * own[SEGMENTS] + (1.0 - is_down) * (1.0 - far[SEGMENTS]))

    keep = jnp.where(me + offset < BLOCKS, 1, 0).astype(F32)

    chip = me // 2

    def put_near(l, total):
        value = (total * keep).astype(BF16)
        first[0, l] = value
        for r in range(BLOCK_CH // TILE):
            m = 2 * (l % LAG_HALF * (BLOCK_CH // TILE) + r) + l // LAG_HALF
            outgoing[m] = value[r * TILE : (r + 1) * TILE]

    for h in range(2):
        lag_sums(0, h, near_copies, put_near)

        def send_part(m):
            pltpu.make_async_remote_copy(
                src_ref=outgoing.at[m], dst_ref=middle.at[me], send_sem=mid_s, recv_sem=mid_r,
                device_id=(m, q), device_id_type=MESH,
            ).start()

        @pl.when(2 * chip + h != me)
        def _():
            send_part(2 * chip + h)

        both_ways(chip, BLOCKS // 2, lambda n: send_part(2 * n + h))
    mid_here = pltpu.make_async_copy(outgoing.at[me], middle.at[me], here_sem.at[2])
    mid_here.start()

    parts = middle.at[pl.ds(0, BLOCKS - 1)]
    mid_here.wait()
    pltpu.make_async_copy(parts, parts, mid_r).wait()

    def stage_part(j, carry):
        onward[j] = middle[wrapped(j - offset, BLOCKS)]
        return carry

    lax.fori_loop(0, BLOCKS, stage_part, 0)
    spot = second.at[
        0, me % 2 * LAG_HALF + me // 2 // 8, pl.ds(pl.multiple_of(me // 2 % 8 * TILE, TILE), TILE)
    ]
    out_here = pltpu.make_async_copy(onward.at[me], spot, here_sem.at[3])
    out_here.start()

    def send_onward(j):
        pltpu.make_async_remote_copy(
            src_ref=onward.at[j], dst_ref=spot, send_sem=out_s, recv_sem=out_r,
            device_id=(j, q), device_id_type=MESH,
        ).start()

    both_ways(me, BLOCKS, send_onward)
    def put_last(l, total):
        sums[l] = total.astype(BF16)

    def hand_over(target, device, h):
        half = pl.ds(h * LAG_HALF, LAG_HALF)
        return pltpu.make_async_remote_copy(
            src_ref=sums.at[half], dst_ref=target.at[1, half], send_sem=sec_s, recv_sem=sec_r,
            device_id=(device, q), device_id_type=MESH,
        )

    for h in range(2):
        lag_sums(1, h, last_copies, put_last)

        @pl.when(down & has_upper)
        def _():
            hand_over(second, upper, h).start()

        @pl.when(~down & has_lower)
        def _():
            hand_over(first, lower, h).start()

    @pl.when(down)
    def _():
        first[1] = sums[...]

    @pl.when(~down)
    def _():
        second[1] = sums[...]

    @pl.when(down & ~has_lower)
    def _():
        second[1] = jnp.zeros_like(sums)

    @pl.when(~down & ~has_upper)
    def _():
        first[1] = jnp.zeros_like(sums)

    out_here.wait()
    pltpu.make_async_copy(parts, parts, out_r).wait()

    @pl.when(gives)
    def _():
        pltpu.make_async_copy(sums, sums, sec_r).wait()

    for t in range(1, PAIRS):
        pltpu.make_async_copy(sixteen, sixteen, ys.at[t]).wait()
    pltpu.make_async_copy(others, others, own_s).wait()
    pltpu.make_async_copy(others, others, near_s).wait()

    @pl.when(gives)
    def _():
        pltpu.make_async_copy(own, own, far_s).wait()

    for copy in last_copies + near_copies:
        copy.wait_send()

    @pl.when(works)
    def _():
        pltpu.make_async_copy(sums, sums, sec_s).wait()

    pltpu.make_async_copy(parts, parts, mid_s).wait()
    pltpu.make_async_copy(parts, parts, out_s).wait()


def correlations(records, offsets, sides):
    hbm = pl.BlockSpec(memory_space=pltpu.HBM)
    vmem = pl.BlockSpec(memory_space=pltpu.VMEM)
    whole = (BLOCKS, ROWS, BLOCK_CH)
    more = (SEGMENTS + 1, ROWS, BLOCK_CH)
    dma = pltpu.SemaphoreType.DMA
    return pl.pallas_call(
        kernel,
        name="correlations",
        out_shape=(
            jax.ShapeDtypeStruct((2, LAG_LOCAL, BLOCK_CH, BLOCK_CH), BF16),
            jax.ShapeDtypeStruct((2, LAG_LOCAL, BLOCK_CH, BLOCK_CH), BF16),
        ),
        in_specs=[hbm] * 6,
        out_specs=(vmem, vmem),
        scratch_shapes=[
            pltpu.VMEM((GROUPS, GROUP * BLOCK_CH, SAMPLES), BF16),
            pltpu.VMEM((4 * BINS, SAMPLES), BF16),
            pltpu.VMEM((LAGS * TILE, ROWS * TILE), BF16),
            pltpu.VMEM((TILE * TILE, TILE * TILE), BF16),
            pltpu.SMEM((2,), jnp.int32),
            pltpu.SMEM((1, 2), jnp.int32),
            pltpu.VMEM((PAIRS, LOCAL_BLOCKS, ROWS, BLOCK_CH), BF16),
            pltpu.VMEM(whole, BF16),
            pltpu.VMEM(whole, BF16),
            pltpu.VMEM(more, BF16),
            pltpu.VMEM(more, BF16),
            pltpu.VMEM(whole, BF16),
            pltpu.VMEM((ROWS, SEGMENTS, BLOCK_CH), BF16),
            pltpu.VMEM((ROWS, SEGMENTS, BLOCK_CH), BF16),
            pltpu.VMEM((ROWS, BLOCK_CH, BLOCK_CH), BF16),
            pltpu.VMEM((2, LAGS, BLOCK_CH, BLOCK_CH), BF16),
            pltpu.VMEM((2, PAIRS, LAG_LOCAL, BLOCK_CH, BLOCK_CH), BF16),
            pltpu.VMEM((BLOCKS, TILE, BLOCK_CH), BF16),
            pltpu.VMEM((BLOCKS, TILE, BLOCK_CH), BF16),
            pltpu.VMEM((BLOCKS, TILE, BLOCK_CH), BF16),
            pltpu.VMEM((LAG_LOCAL, BLOCK_CH, BLOCK_CH), BF16),
            dma((GROUPS,)), dma((5,)), dma((PAIRS,)), dma((PAIRS, GROUPS)),
            dma, dma, dma, dma, dma, dma, dma((4,)), dma((2, PAIRS, 2)), dma((2, PAIRS, 2)), dma, dma,
            dma, dma, dma, dma,
        ],
        compiler_params=pltpu.CompilerParams(
            collective_id=0, has_side_effects=True, vmem_limit_bytes=62 * 1024 * 1024
        ),
    )(records, jnp.asarray(fourier_rows()), jnp.asarray(lag_rows()), jnp.asarray(swap_rows()), offsets, sides)


def local(records, offsets, sides):
    first, second = correlations(records, offsets, sides)
    return first[None], second[None]


def solution(mesh):
    return jax.shard_map(
        local,
        mesh=mesh,
        in_specs=(P("blk", "pair", None), P(), P("blk", None)),
        out_specs=(P("blk", None, "pair", None, None), P("blk", None, "pair", None, None)),
        check_vma=False,
    )
```

```python
import functools
import math

import jax
import jax.numpy as jnp
import numpy as np
from jax import lax
from jax.experimental import pallas as pl
from jax.experimental.pallas import tpu as pltpu
from jax.sharding import PartitionSpec as P

BLOCK_CH = 128
BINS = 128
SAMPLES = 2048
FIRST_BIN = 4
LAGS = 32
SEGMENTS = 64
BLOCKS = 64
LAST_OFFSET = 15
PAIRS = 4
BIN_LOCAL = BINS // PAIRS
ROWS = 2 * BIN_LOCAL
LAG_LOCAL = LAGS // PAIRS
LAG_HALF = LAG_LOCAL // 2
LOCAL_BLOCKS = BLOCKS // PAIRS
GROUP = 2
GROUPS = LOCAL_BLOCKS // GROUP
BEHIND = 6
TILE = 16
BF16 = jnp.bfloat16
F32 = jnp.float32
MESH = pl.DeviceIdType.MESH


def fourier_rows():
    n = np.arange(SAMPLES, dtype=np.int64)
    k = FIRST_BIN + np.arange(BINS, dtype=np.int64)
    angles = 2.0 * math.pi / SAMPLES * (k[:, None] * n[None, :] % SAMPLES).astype(np.float64)
    taper = 0.5 - 0.5 * np.cos(2.0 * math.pi / SAMPLES * n.astype(np.float64))
    table = np.stack((taper * np.cos(angles), -taper * np.sin(angles)))
    table = table.reshape(2, PAIRS, BIN_LOCAL, SAMPLES).transpose(1, 0, 2, 3).reshape(2 * BINS, SAMPLES)
    high = table.astype(BF16)
    low = (table - high.astype(np.float64)).astype(BF16)
    return np.concatenate((high, low), axis=0)


def lag_rows():
    lag = np.arange(LAGS, dtype=np.int64) - LAGS // 2
    k = FIRST_BIN + np.arange(BINS, dtype=np.int64)
    angles = 2.0 * math.pi / SAMPLES * (lag[:, None] * k[None, :] % SAMPLES).astype(np.float64)
    table = np.stack((np.cos(angles), -np.sin(angles))) / math.sqrt(SEGMENTS * BINS)
    table = table.reshape(2, LAGS, PAIRS, BIN_LOCAL).transpose(2, 1, 0, 3).reshape(PAIRS, LAGS, ROWS)
    same = np.eye(TILE)
    spread = table[:, :, None, :, None] * same[None, None, :, None, :]
    return spread.reshape(PAIRS, LAGS * TILE, ROWS * TILE).astype(BF16)


def swap_rows():
    index = np.arange(TILE * TILE)
    table = np.zeros((TILE * TILE, TILE * TILE))
    table[index, (index % TILE) * TILE + index // TILE] = 1.0
    return table.astype(BF16)


def kernel(
    records, fourier, lagtab, swap, offsets_h, sides_h,
    first, second,
    rec_v, fourier_v, lagtab_v, swap_v, offsets, sides,
    shares, spectra, staged, own, far, near, own_t, far_t, cross, lagged, arrived, middle, onward, outgoing, sums,
    load_sem, table_sem, ys, yr, own_s, own_r, near_s, near_r, far_s, far_r, here_sem, lag_s, lag_r, sec_s, sec_r,
    mid_s, mid_r, out_s, out_r,
):
    me = lax.axis_index("blk")
    q = lax.axis_index("pair")
    barrier = pltpu.get_barrier_semaphore()

    loads = []
    table_loads = [
        pltpu.make_async_copy(fourier, fourier_v, table_sem.at[0]),
        pltpu.make_async_copy(swap, swap_v, table_sem.at[1]),
        pltpu.make_async_copy(lagtab.at[q], lagtab_v, table_sem.at[2]),
        pltpu.make_async_copy(offsets_h, offsets, table_sem.at[3]),
        pltpu.make_async_copy(sides_h, sides, table_sem.at[4]),
    ]
    table_loads[0].start()
    width = GROUP * BLOCK_CH
    place = lax.rem(me // 2, GROUPS)

    def turn_of(g):
        ahead = (g % 2) * ((g + 1) // 2) + (1 - g % 2) * (GROUPS - g // 2)
        return lax.rem(place + GROUPS // 2 + ahead, GROUPS)

    for g in range(GROUPS):
        row = pl.multiple_of(turn_of(g) * width, width)
        copy = pltpu.make_async_copy(records.at[0, pl.ds(row, width)], rec_v.at[g], load_sem.at[g])
        copy.start()
        loads.append(copy)
    for copy in table_loads[1:]:
        copy.start()

    def wrapped(value, count):
        value = jnp.where(value >= count, value - count, value)
        return jnp.where(value < 0, value + count, value)

    def both_ways(here, count, send):
        def step(t, carry):
            send(wrapped(here + count // 2 - t, count))
            send(wrapped(here - count // 2 + t, count))
            return carry

        send(wrapped(here + count // 2, count))
        lax.fori_loop(1, count // 2, step, 0)

    def greet(b):
        pl.semaphore_signal(barrier, inc=1, device_id=(b, q), device_id_type=MESH)

    both_ways(me, BLOCKS, greet)
    for t in range(1, PAIRS):
        pl.semaphore_signal(barrier, inc=1, device_id=(me, lax.rem(q + t, PAIRS)), device_id_type=MESH)

    def whiten(g):
        out = lax.dot_general(
            fourier_v[...], rec_v[g], (((1,), (1,)), ((), ())), preferred_element_type=F32
        )
        spectrum = (out[: 2 * BINS] + out[2 * BINS :]).reshape(PAIRS, 2, BIN_LOCAL, width)
        at = turn_of(g) * GROUP
        power = spectrum[:, 0] * spectrum[:, 0] + spectrum[:, 1] * spectrum[:, 1]
        for i in range(GROUP):
            lanes = slice(i * BLOCK_CH, (i + 1) * BLOCK_CH)
            level = jnp.sum(power[:, :, lanes], axis=-1, keepdims=True) * (1.0 / BLOCK_CH)
            scale = 1.0 / jnp.sqrt(level + 1e-05)
            white = (spectrum[:, :, :, lanes] * scale[:, None]).astype(BF16)
            shares[:, at + i] = white.reshape(PAIRS, ROWS, BLOCK_CH)
            spectra[q * LOCAL_BLOCKS + at + i] = shares[q, at + i]

    def send_block(source, target, b, send_sem, recv_sem):
        @pl.when(b != me)
        def _():
            pltpu.make_async_remote_copy(
                src_ref=source.at[b], dst_ref=target.at[me], send_sem=send_sem, recv_sem=recv_sem,
                device_id=(b, q), device_id_type=MESH,
            ).start()

    def send_group(g):
        at = turn_of(g) * GROUP
        for t in (2, 1, 3):
            peer = lax.rem(q + t, PAIRS)
            pltpu.make_async_remote_copy(
                src_ref=shares.at[peer, pl.ds(at, GROUP)],
                dst_ref=spectra.at[pl.ds(q * LOCAL_BLOCKS + at, GROUP)],
                send_sem=ys.at[t], recv_sem=yr.at[t, g],
                device_id=(me, peer), device_id_type=MESH,
            ).start()
        for i in range(GROUP):
            send_block(spectra, own, q * LOCAL_BLOCKS + at + i, own_s, own_r)

    def pass_on(g):
        at = turn_of(g) * GROUP
        two = spectra.at[pl.ds(0, GROUP)]
        for t in (1, 3, 2):
            pltpu.make_async_copy(two, two, yr.at[t, g]).wait()
            base = lax.rem(q + PAIRS - t, PAIRS) * LOCAL_BLOCKS
            for i in range(GROUP):
                send_block(spectra, own, base + at + i, own_s, own_r)

    table_loads[0].wait()
    loads[0].wait()
    whiten(0)
    pl.semaphore_wait(barrier, BLOCKS - 1 + PAIRS - 1)
    send_group(0)
    for g in range(1, GROUPS):
        loads[g].wait()

    def group_step(g, carry):
        whiten(g)
        send_group(g)
        return carry

    def late_step(g, carry):
        whiten(g)
        send_group(g)
        pass_on(g - BEHIND)
        return carry

    def pass_step(g, carry):
        pass_on(g)
        return carry

    lax.fori_loop(1, BEHIND, group_step, 0)
    lax.fori_loop(BEHIND, GROUPS, late_step, 0)
    lax.fori_loop(GROUPS - BEHIND, GROUPS, pass_step, 0)
    sixteen = spectra.at[pl.ds(0, LOCAL_BLOCKS)]
    own_here = pltpu.make_async_copy(spectra.at[me], own.at[me], here_sem.at[0])
    own_here.start()

    for copy in table_loads[1:]:
        copy.wait()
    offset = offsets[0]

    def stage(b, carry):
        staged[b] = spectra[jnp.minimum(b + offset, BLOCKS - 1)]
        return carry

    lax.fori_loop(0, BLOCKS, stage, 0)
    near_here = pltpu.make_async_copy(staged.at[me], near.at[me], here_sem.at[1])
    near_here.start()

    def send_staged(b):
        pltpu.make_async_remote_copy(
            src_ref=staged.at[b], dst_ref=near.at[me], send_sem=near_s, recv_sem=near_r,
            device_id=(b, q), device_id_type=MESH,
        ).start()

    both_ways(me, BLOCKS, send_staged)

    others = own.at[pl.ds(0, BLOCKS - 1)]
    own_here.wait()
    pltpu.make_async_copy(others, others, own_r).wait()
    down = me % LAST_OFFSET % 2 == 0
    has_lower = me >= LAST_OFFSET
    has_upper = me + LAST_OFFSET < BLOCKS
    lower = lax.rem(me + BLOCKS - LAST_OFFSET, BLOCKS)
    upper = lax.rem(me + LAST_OFFSET, BLOCKS)
    gives = (down & has_lower) | (~down & has_upper)
    works = (down & has_upper) | (~down & has_lower)
    own[SEGMENTS] = jnp.full((ROWS, BLOCK_CH), sides[0, 1].astype(F32), F32).astype(BF16)
    receiver = jnp.where(down, lower, upper)

    def forward(start, count):
        piece = pl.ds(start, count)
        return pltpu.make_async_remote_copy(
            src_ref=own.at[piece], dst_ref=far.at[piece], send_sem=far_s, recv_sem=far_r,
            device_id=(receiver, q), device_id_type=MESH,
        )

    @pl.when(gives)
    def _():
        for start, count in ((0, 16), (16, 16), (32, 16), (48, 17)):
            forward(start, count).start()

    def turn(source, target):
        for i in range(SEGMENTS // TILE):
            for j in range(0, ROWS // TILE, 2):
                segs = slice(i * TILE, (i + 1) * TILE)
                rows = [slice((j + n) * TILE, (j + n + 1) * TILE) for n in range(2)]
                tiles = [source[segs, row, :].reshape(TILE * TILE, BLOCK_CH) for row in rows]
                turned = jnp.dot(swap_v[...], jnp.concatenate(tiles, axis=1), preferred_element_type=F32).astype(BF16)
                for n in range(2):
                    lanes = slice(n * BLOCK_CH, (n + 1) * BLOCK_CH)
                    target[rows[n], segs, :] = turned[:, lanes].reshape(TILE, TILE, BLOCK_CH)

    turn(own, own_t)

    def correlate(k, swapped):
        straight = 1.0 - swapped

        def bin_step(f, carry):
            own_re, own_im = own_t[f], own_t[BIN_LOCAL + f]
            far_re, far_im = far_t[f], far_t[BIN_LOCAL + f]
            src_re = own_re * straight + far_re * swapped
            src_im = own_im * straight + far_im * swapped
            rec_re = far_re * straight + own_re * swapped
            rec_im = far_im * straight + own_im * swapped
            left = jnp.concatenate((src_re, src_im), axis=0)
            right = jnp.concatenate(
                (jnp.concatenate((rec_re, rec_im), axis=0), jnp.concatenate((rec_im, -rec_re), axis=0)), axis=1
            )
            out = lax.dot_general(left, right, (((0,), (0,)), ((), ())), preferred_element_type=F32)
            cross[f] = out[:, :BLOCK_CH].astype(BF16)
            cross[BIN_LOCAL + f] = out[:, BLOCK_CH:].astype(BF16)
            return carry

        lax.fori_loop(0, BIN_LOCAL, bin_step, 0, unroll=4)

        def lag_step(i, carry):
            c0 = pl.multiple_of(i * 2 * TILE, 2 * TILE)
            c1 = pl.multiple_of(i * 2 * TILE + TILE, TILE)
            cols = jnp.concatenate(
                (
                    cross[:, pl.ds(c0, TILE), :].reshape(ROWS * TILE, BLOCK_CH),
                    cross[:, pl.ds(c1, TILE), :].reshape(ROWS * TILE, BLOCK_CH),
                ),
                axis=1,
            )
            out = jnp.dot(lagtab_v[...], cols, preferred_element_type=F32).astype(BF16)
            lagged[k, :, pl.ds(c0, TILE), :] = out[:, :BLOCK_CH].reshape(LAGS, TILE, BLOCK_CH)
            lagged[k, :, pl.ds(c1, TILE), :] = out[:, BLOCK_CH:].reshape(LAGS, TILE, BLOCK_CH)
            return carry

        lax.fori_loop(0, BLOCK_CH // (2 * TILE), lag_step, 0, unroll=4)
        copies = []
        for h in range(2):
            for t in (2, 1, 3):
                peer = lax.rem(q + t, PAIRS)
                copy = pltpu.make_async_remote_copy(
                    src_ref=lagged.at[k, pl.ds(peer * LAG_LOCAL + h * LAG_HALF, LAG_HALF)],
                    dst_ref=arrived.at[k, t, pl.ds(h * LAG_HALF, LAG_HALF)],
                    send_sem=lag_s.at[k, t, h], recv_sem=lag_r.at[k, t, h],
                    device_id=(me, peer), device_id_type=MESH,
                )
                copy.start()
                copies.append(copy)
        return copies

    def lag_sums(k, h, copies, put):
        for copy in copies[h * (PAIRS - 1) : (h + 1) * (PAIRS - 1)]:
            copy.wait_recv()

        for l in range(h * LAG_HALF, (h + 1) * LAG_HALF):
            total = lagged[k, q * LAG_LOCAL + l].astype(F32)
            for t in range(1, PAIRS):
                total = total + arrived[k, t, l].astype(F32)
            put(l, total)

    near_here.wait()
    pltpu.make_async_copy(others, others, near_r).wait()
    turn(near, far_t)
    near_copies = correlate(0, jnp.full((SEGMENTS, BLOCK_CH), sides[0, 0].astype(F32), F32).astype(BF16))

    @pl.when(works)
    def _():
        pltpu.make_async_copy(far, far, far_r).wait()

    @pl.when(~works)
    def _():
        far[...] = jnp.zeros_like(far)

    turn(far, far_t)
    is_down = jnp.full((SEGMENTS, BLOCK_CH), jnp.where(down, 1, 0).astype(F32), F32).astype(BF16)
    last_copies = correlate(1, is_down * own[SEGMENTS] + (1.0 - is_down) * (1.0 - far[SEGMENTS]))

    keep = jnp.where(me + offset < BLOCKS, 1, 0).astype(F32)

    chip = me // 2

    def put_near(l, total):
        value = (total * keep).astype(BF16)
        first[0, l] = value
        for r in range(BLOCK_CH // TILE):
            m = 2 * (l % LAG_HALF * (BLOCK_CH // TILE) + r) + l // LAG_HALF
            outgoing[m] = value[r * TILE : (r + 1) * TILE]

    for h in range(2):
        lag_sums(0, h, near_copies, put_near)

        def send_part(m):
            pltpu.make_async_remote_copy(
                src_ref=outgoing.at[m], dst_ref=middle.at[me], send_sem=mid_s, recv_sem=mid_r,
                device_id=(m, q), device_id_type=MESH,
            ).start()

        @pl.when(2 * chip + h != me)
        def _():
            send_part(2 * chip + h)

        both_ways(chip, BLOCKS // 2, lambda n: send_part(2 * n + h))
    mid_here = pltpu.make_async_copy(outgoing.at[me], middle.at[me], here_sem.at[2])
    mid_here.start()

    parts = middle.at[pl.ds(0, BLOCKS - 1)]
    mid_here.wait()
    pltpu.make_async_copy(parts, parts, mid_r).wait()

    def stage_part(j, carry):
        onward[j] = middle[wrapped(j - offset, BLOCKS)]
        return carry

    lax.fori_loop(0, BLOCKS, stage_part, 0)
    spot = second.at[
        0, me % 2 * LAG_HALF + me // 2 // 8, pl.ds(pl.multiple_of(me // 2 % 8 * TILE, TILE), TILE)
    ]
    out_here = pltpu.make_async_copy(onward.at[me], spot, here_sem.at[3])
    out_here.start()

    def send_onward(j):
        pltpu.make_async_remote_copy(
            src_ref=onward.at[j], dst_ref=spot, send_sem=out_s, recv_sem=out_r,
            device_id=(j, q), device_id_type=MESH,
        ).start()

    both_ways(me, BLOCKS, send_onward)
    def put_last(l, total):
        sums[l] = total.astype(BF16)

    def hand_over(target, device, h):
        half = pl.ds(h * LAG_HALF, LAG_HALF)
        return pltpu.make_async_remote_copy(
            src_ref=sums.at[half], dst_ref=target.at[1, half], send_sem=sec_s, recv_sem=sec_r,
            device_id=(device, q), device_id_type=MESH,
        )

    for h in range(2):
        lag_sums(1, h, last_copies, put_last)

        @pl.when(down & has_upper)
        def _():
            hand_over(second, upper, h).start()

        @pl.when(~down & has_lower)
        def _():
            hand_over(first, lower, h).start()

    @pl.when(down)
    def _():
        first[1] = sums[...]

    @pl.when(~down)
    def _():
        second[1] = sums[...]

    @pl.when(down & ~has_lower)
    def _():
        second[1] = jnp.zeros_like(sums)

    @pl.when(~down & ~has_upper)
    def _():
        first[1] = jnp.zeros_like(sums)

    out_here.wait()
    pltpu.make_async_copy(parts, parts, out_r).wait()

    @pl.when(gives)
    def _():
        pltpu.make_async_copy(sums, sums, sec_r).wait()

    for t in range(1, PAIRS):
        pltpu.make_async_copy(sixteen, sixteen, ys.at[t]).wait()
    pltpu.make_async_copy(others, others, own_s).wait()
    pltpu.make_async_copy(others, others, near_s).wait()

    @pl.when(gives)
    def _():
        pltpu.make_async_copy(own, own, far_s).wait()

    for copy in last_copies + near_copies:
        copy.wait_send()

    @pl.when(works)
    def _():
        pltpu.make_async_copy(sums, sums, sec_s).wait()

    pltpu.make_async_copy(parts, parts, mid_s).wait()
    pltpu.make_async_copy(parts, parts, out_s).wait()


def correlations(records, offsets, sides):
    hbm = pl.BlockSpec(memory_space=pltpu.HBM)
    vmem = pl.BlockSpec(memory_space=pltpu.VMEM)
    whole = (BLOCKS, ROWS, BLOCK_CH)
    more = (SEGMENTS + 1, ROWS, BLOCK_CH)
    dma = pltpu.SemaphoreType.DMA
    return pl.pallas_call(
        kernel,
        name="correlations",
        out_shape=(
            jax.ShapeDtypeStruct((2, LAG_LOCAL, BLOCK_CH, BLOCK_CH), BF16),
            jax.ShapeDtypeStruct((2, LAG_LOCAL, BLOCK_CH, BLOCK_CH), BF16),
        ),
        in_specs=[hbm] * 6,
        out_specs=(vmem, vmem),
        scratch_shapes=[
            pltpu.VMEM((GROUPS, GROUP * BLOCK_CH, SAMPLES), BF16),
            pltpu.VMEM((4 * BINS, SAMPLES), BF16),
            pltpu.VMEM((LAGS * TILE, ROWS * TILE), BF16),
            pltpu.VMEM((TILE * TILE, TILE * TILE), BF16),
            pltpu.SMEM((2,), jnp.int32),
            pltpu.SMEM((1, 2), jnp.int32),
            pltpu.VMEM((PAIRS, LOCAL_BLOCKS, ROWS, BLOCK_CH), BF16),
            pltpu.VMEM(whole, BF16),
            pltpu.VMEM(whole, BF16),
            pltpu.VMEM(more, BF16),
            pltpu.VMEM(more, BF16),
            pltpu.VMEM(whole, BF16),
            pltpu.VMEM((ROWS, SEGMENTS, BLOCK_CH), BF16),
            pltpu.VMEM((ROWS, SEGMENTS, BLOCK_CH), BF16),
            pltpu.VMEM((ROWS, BLOCK_CH, BLOCK_CH), BF16),
            pltpu.VMEM((2, LAGS, BLOCK_CH, BLOCK_CH), BF16),
            pltpu.VMEM((2, PAIRS, LAG_LOCAL, BLOCK_CH, BLOCK_CH), BF16),
            pltpu.VMEM((BLOCKS, TILE, BLOCK_CH), BF16),
            pltpu.VMEM((BLOCKS, TILE, BLOCK_CH), BF16),
            pltpu.VMEM((BLOCKS, TILE, BLOCK_CH), BF16),
            pltpu.VMEM((LAG_LOCAL, BLOCK_CH, BLOCK_CH), BF16),
            dma((GROUPS,)), dma((5,)), dma((PAIRS,)), dma((PAIRS, GROUPS)),
            dma, dma, dma, dma, dma, dma, dma((4,)), dma((2, PAIRS, 2)), dma((2, PAIRS, 2)), dma, dma,
            dma, dma, dma, dma,
        ],
        compiler_params=pltpu.CompilerParams(
            collective_id=0, has_side_effects=True, vmem_limit_bytes=62 * 1024 * 1024
        ),
    )(records, jnp.asarray(fourier_rows()), jnp.asarray(lag_rows()), jnp.asarray(swap_rows()), offsets, sides)


def local(records, offsets, sides):
    first, second = correlations(records, offsets, sides)
    return first[None], second[None]


def solution(mesh):
    return jax.shard_map(
        local,
        mesh=mesh,
        in_specs=(P("blk", "pair", None), P(), P("blk", None)),
        out_specs=(P("blk", None, "pair", None, None), P("blk", None, "pair", None, None)),
        check_vma=False,
    )
```
